32 devices in a mesh: groups: 2 (over x), seq: 16 (over z, y, core).
Axes of the slice: x: 2, y: 2, z: 4, core: 2. Of those that a mesh axis runs over, the one named last changes fastest.
Arguments:
- points: bfloat16 [32768, 1024], P(('groups', 'seq')), parts along dimension 0, may hold values from -110 to 110
- in_weight: bfloat16 [1024, 1536], P('seq'), may hold values from -0.1875 to 0.1875
- slice_token_weight: float32 [3, 64, 64], replicated, may hold values from -0.75 to 0.75
- cotangent: bfloat16 [32768, 1024], P(('groups', 'seq')), parts along dimension 0, may hold values from -48 to 48
Outputs:
- grad_points: bfloat16 [32768, 1024], P(('groups', 'seq')), parts along dimension 0
- grad_in_weight: float32 [2048, 1536], P(('groups', 'seq')), parts along dimension 0
- grad_token_weights: float32 [6, 64, 64], P('groups'), parts along dimension 0
The draws below stay inside these ranges and needn't reach their ends.
There are 2 independent parts, one for each index of `groups`. The reference program is written for one: setup_inputs(seed, part) draws one part's arguments, and reference() takes and returns one part's arrays. A program takes and returns all parts, laid end to end along the dimension named above; an argument that names none is the same for every part. Nothing has to cross between parts.
All inputs are finite; a program needn't handle non-finite values.
Results may differ from the reference program's by a relative error of at most 0.012.
Values may be sent and summed in bfloat16 or wider, within the bound.
A program may use at most 128 MiB of HBM per device.

```python
import jax
import jax.numpy as jnp
from jax import lax

D = 1024
H = 16
M = 32
DH = 64
TOKENS = 16384


def weld_profiles(key):
    phases = jax.random.uniform(jax.random.fold_in(key, 11), (4,), jnp.float32, 0.0, 6.2831855)
    position = (jnp.arange(TOKENS, dtype=jnp.float32) + 0.5) / TOKENS
    return [jnp.cos(3.1415927 * (order + 1) * position + phases[order]) * 1.4142135 for order in range(4)]


def along_profiles(profiles, directions):
    summed = profiles[0][:, None] * directions[0][None, :]
    for order in range(1, 4):
        summed = summed + profiles[order][:, None] * directions[order][None, :]
    return summed


def draw_points(key, part):
    profiles = weld_profiles(key)
    key = jax.random.fold_in(key, 7)
    noise_key = jax.random.fold_in(key, 0)
    direction_key = jax.random.fold_in(key, 4)
    directions = jax.random.normal(direction_key, (4, D), jnp.float32)
    offset = along_profiles(profiles, directions)
    values = jnp.clip(jax.random.normal(noise_key, (TOKENS, D), jnp.float32), -6.0, 6.0) + offset
    return jnp.clip(values, -110.0, 110.0).astype(jnp.bfloat16)


def draw_cotangent(key, part):
    profiles = weld_profiles(key)
    key = jax.random.fold_in(key, 9)
    noise_key, direction_key = jax.random.split(key, 2)
    directions = jax.random.normal(direction_key, (4, D), jnp.float32) * 2.0
    offset = along_profiles(profiles, directions)
    values = jnp.clip(jax.random.normal(noise_key, (TOKENS, D), jnp.float32) * 8.0, -40.0, 40.0) + offset
    return jnp.clip(values, -48.0, 48.0).astype(jnp.bfloat16)


def shard_levels(key, extent, pieces, smallest, high):
    level, own = 1.0, jax.random.fold_in(key, 6)
    for dim, shards_of in pieces:
        heights = jnp.exp(jax.random.uniform(jax.random.fold_in(own, dim), (shards_of,), jnp.float32, smallest / len(pieces), high / len(pieces)))
        level = level * jnp.repeat(heights, extent[dim] // shards_of).reshape([-1 if axis == dim else 1 for axis in range(len(extent))])
    return level


def normal_values(stream_key, shape, scale, reach, cuts=(), kind=jnp.bfloat16):
    factor_of = shard_levels(stream_key, shape, cuts, -0.22, 0.18) if cuts else 1.0
    drawn = jax.random.normal(stream_key, shape, jnp.float32) * scale * factor_of
    return jnp.minimum(jnp.maximum(drawn, -reach), reach).astype(kind)


def setup_inputs(seed: int = 0, part: int = 0) -> dict:
    key_of = jax.random.split(jax.random.key(seed), 5)
    part_splits = jax.random.split(jax.random.fold_in(key_of[4], part), 5)
    points = draw_points(jax.random.fold_in(jax.random.fold_in(key_of[4], part), 71), part)
    in_weight = normal_values(key_of[1], (D, D + H * M), D ** -0.5, 0.1875, ((0, 16),))
    slice_token_weight = normal_values(key_of[2], (3, DH, DH), DH ** -0.5, 0.75, (), jnp.float32)
    cotangent = draw_cotangent(jax.random.fold_in(jax.random.fold_in(key_of[4], part), 71), part)
    return {"points": points, "in_weight": in_weight, "slice_token_weight": slice_token_weight, "cotangent": cotangent}


def token_mixing(slice_tokens, slice_token_weight):
    highest_precision = lax.Precision.HIGHEST
    query_rows = jnp.einsum('pat,tg->pag', slice_tokens, slice_token_weight[0], precision=highest_precision)
    key_matrix = jnp.einsum('pat,tg->pag', slice_tokens, slice_token_weight[1], precision=highest_precision)
    value_matrix = jnp.einsum('pat,tg->pag', slice_tokens, slice_token_weight[2], precision=highest_precision)
    scores = jnp.einsum('hme,hke->hmk', query_rows, key_matrix, precision=highest_precision) / jnp.sqrt(jnp.float32(DH))
    attend = jax.nn.softmax(scores, axis=-1)
    return jnp.einsum('hmk,hke->hme', attend, value_matrix, precision=highest_precision)

def reference(points, in_weight, slice_token_weight, cotangent):
    count = points.shape[0]
    projected = jnp.dot(points, in_weight, preferred_element_type=jnp.float32)
    point_features = projected[:, :D].astype(jnp.bfloat16).reshape(count, H, DH)
    soft = jax.nn.softmax(projected[:, D:].reshape(count, H, M), axis=-1)
    backward_softmax = soft.astype(jnp.bfloat16)
    forward_softmax = backward_softmax.astype(jnp.float32)
    mass = lax.optimization_barrier(jnp.sum(forward_softmax, axis=0))
    slice_totals = jnp.einsum('uog,uoa->oga', forward_softmax, point_features.astype(jnp.float32))
    denom = mass + 1e-05
    slice_tokens = slice_totals / denom[:, :, None]
    mixed, mix_vjp = jax.vjp(token_mixing, slice_tokens, slice_token_weight)
    backward_mixed_tokens = mixed.astype(jnp.bfloat16).astype(jnp.float32)
    forward_gradient = cotangent.reshape(count, H, DH).astype(jnp.float32)
    mixed_tokens_gradient = jnp.einsum('uog,uoa->oga', forward_softmax, forward_gradient)
    d_tokens, grad_token_weights = mix_vjp(mixed_tokens_gradient)
    slice_totals_gradient = (d_tokens / denom[:, :, None]).astype(jnp.bfloat16).astype(jnp.float32)
    slice_mass_gradient = -lax.optimization_barrier(jnp.sum(d_tokens * slice_tokens, axis=-1)) / denom
    softmax_gradient = jnp.einsum('ugv,gfv->ugf', forward_gradient, backward_mixed_tokens)
    softmax_gradient = softmax_gradient + jnp.einsum('ugv,gfv->ugf', point_features.astype(jnp.float32), slice_totals_gradient) + slice_mass_gradient[None]
    d_logits = soft * (softmax_gradient - lax.optimization_barrier(jnp.sum(soft * softmax_gradient, axis=-1, keepdims=True)))
    feature_gradient = jnp.einsum('lvt,vtz->lvz', forward_softmax, slice_totals_gradient)
    grads = jnp.concatenate([feature_gradient.reshape(count, D), d_logits.reshape(count, H * M)], axis=1).astype(jnp.bfloat16)
    grad_points = lax.dot_general(grads, in_weight, (((1,), (1,)), ((), ())), preferred_element_type=jnp.float32).astype(jnp.bfloat16)
    grad_in_weight = lax.dot_general(points, grads, (((0,), (0,)), ((), ())), preferred_element_type=jnp.float32)
    return (grad_points, grad_in_weight, grad_token_weights)
```

```python
import jax
import jax.numpy as jnp
from jax import lax
from jax.experimental import pallas as pl
from jax.experimental.pallas import tpu as pltpu
from jax.sharding import PartitionSpec as P

D = 1024
H = 16
M = 32
DH = 64


def token_mixing(slice_tokens, slice_token_weight):
    highest_precision = lax.Precision.HIGHEST
    query_rows = jnp.einsum(
        "pat,tg->pag", slice_tokens, slice_token_weight[0], precision=highest_precision
    )
    key_matrix = jnp.einsum(
        "pat,tg->pag", slice_tokens, slice_token_weight[1], precision=highest_precision
    )
    value_matrix = jnp.einsum(
        "pat,tg->pag", slice_tokens, slice_token_weight[2], precision=highest_precision
    )
    scores = jnp.einsum(
        "hme,hke->hmk", query_rows, key_matrix, precision=highest_precision
    ) / jnp.sqrt(jnp.float32(DH))
    attend = jax.nn.softmax(scores, axis=-1)
    return jnp.einsum("hmk,hke->hme", attend, value_matrix, precision=highest_precision)


def local(points, in_weight, slice_token_weight, cotangent):
    count = points.shape[0]
    whole_weight = lax.all_gather(in_weight, "seq", axis=0, tiled=True)
    projected = jnp.dot(points, whole_weight, preferred_element_type=jnp.float32)
    point_features = projected[:, :D].astype(jnp.bfloat16).reshape(count, H, DH)
    soft = jax.nn.softmax(projected[:, D:].reshape(count, H, M), axis=-1)
    backward_softmax = soft.astype(jnp.bfloat16)
    backward_gradient = cotangent.reshape(count, H, DH)
    mass = jnp.sum(backward_softmax.astype(jnp.float32), axis=0)
    slice_totals = jnp.einsum(
        "uog,uoa->oga", backward_softmax, point_features, preferred_element_type=jnp.float32
    )
    mass, slice_totals = lax.psum((mass, slice_totals), "seq")
    denom = mass + 1e-05
    slice_tokens = slice_totals / denom[:, :, None]
    mixed, mix_vjp = jax.vjp(token_mixing, slice_tokens, slice_token_weight)
    backward_mixed_tokens = mixed.astype(jnp.bfloat16)
    local_mixed_tokens = jnp.einsum(
        "uog,uoa->oga", backward_softmax, backward_gradient, preferred_element_type=jnp.float32
    )
    mixed_tokens_gradient = lax.psum(local_mixed_tokens, "seq")
    d_tokens, grad_token_weights = mix_vjp(mixed_tokens_gradient)
    slice_totals_gradient = (d_tokens / denom[:, :, None]).astype(jnp.bfloat16)
    slice_mass_gradient = -jnp.sum(d_tokens * slice_tokens, axis=-1) / denom
    softmax_gradient = jnp.einsum(
        "ugv,gfv->ugf", backward_gradient, backward_mixed_tokens, preferred_element_type=jnp.float32
    )
    softmax_gradient = (
        softmax_gradient
        + jnp.einsum(
            "ugv,gfv->ugf",
            point_features,
            slice_totals_gradient,
            preferred_element_type=jnp.float32,
        )
        + slice_mass_gradient[None]
    )
    d_logits = soft * (softmax_gradient - jnp.sum(soft * softmax_gradient, axis=-1, keepdims=True))
    feature_gradient = jnp.einsum(
        "lvt,vtz->lvz", backward_softmax, slice_totals_gradient, preferred_element_type=jnp.float32
    )
    grads = jnp.concatenate(
        [feature_gradient.reshape(count, D), d_logits.reshape(count, H * M)], axis=1
    ).astype(jnp.bfloat16)
    back = lax.dot_general(
        grads, whole_weight, (((1,), (1,)), ((), ())), preferred_element_type=jnp.float32
    )
    grad_points = back.astype(jnp.bfloat16)
    grad_in_weight = lax.psum_scatter(
        lax.dot_general(
            points, grads, (((0,), (0,)), ((), ())), preferred_element_type=jnp.float32
        ),
        "seq",
        scatter_dimension=0,
        tiled=True,
    )
    return (grad_points, grad_in_weight, grad_token_weights)


MESH = pl.DeviceIdType.MESH
F32 = jnp.float32
BF16 = jnp.bfloat16
HIGHEST = lax.Precision.HIGHEST
N = 16
Z = 4
ROWS = D // N
WIDTH = D + H * M


def dot(a, b, dims=(1, 0), precision=None):
    return lax.dot_general(
        a, b, (((dims[0],), (dims[1],)), ((), ())), precision=precision, preferred_element_type=F32
    )


def kernel(
    points, win, tw, cot, gp, gw, gtw,
    w, pts_t, feat, soft, softb, stat, rbuf, full, dsum_m, mix_m, dmass, grads,
    part, keep, cbuf, crbuf, ybuf, yrbuf, zbuf, zrbuf,
    gsend, grecv, ssend, srecv, csend, crecv, ysend, yrecv, zsend, zrecv,
):
    count = points.shape[0]
    tile = 256
    me = lax.axis_index("seq")
    z, y, c = me // 4, (me // 2) % 2, me % 2

    def device(zz, yy, cc):
        return (zz * 2 + yy) * 2 + cc

    sibling, across = device(z, y, 1 - c), device(z, 1 - y, c)

    def remote(src, dst, send, recv, to):
        return pltpu.make_async_remote_copy(
            src_ref=src, dst_ref=dst, send_sem=send, recv_sem=recv,
            device_id={"seq": to}, device_id_type=MESH,
        )

    barrier = pltpu.get_barrier_semaphore()

    @pl.loop(1, N)
    def _(k):
        pl.semaphore_signal(
            barrier, inc=1, device_id={"seq": lax.rem(me + k, N)}, device_id_type=MESH
        )

    w[me] = win[...]
    pl.semaphore_wait(barrier, N - 1)

    def block(blk, slot, to):
        return remote(w.at[blk], w.at[blk], gsend.at[slot, blk], grecv.at[blk], to)

    up = jnp.minimum(z + 1, Z - 1)
    down = jnp.maximum(z - 1, 0)
    to_up, to_down = device(up, y, c), device(down, y, c)

    def spread(blk):
        block(blk, 2, across).start()
        block(blk, 3, sibling).start()

    @pl.when(z < Z - 1)
    def _():
        block(me, 0, to_up).start()

    @pl.when(z > 0)
    def _():
        block(me, 1, to_down).start()

    spread(me)

    for k in range(D // tile):
        cols = slice(k * tile, (k + 1) * tile)
        pts_t[cols, :] = points[:, cols].T

    for d in range(1, Z):
        @pl.when(z - d >= 0)
        def _():
            blk = device(z - d, y, c)
            block(blk, 0, to_up).wait_recv()

            @pl.when(z < Z - 1)
            def _():
                block(blk, 0, to_up).start()

            spread(blk)

        @pl.when(z + d < Z)
        def _():
            blk = device(z + d, y, c)
            block(blk, 1, to_down).wait_recv()

            @pl.when(z > 0)
            def _():
                block(blk, 1, to_down).start()

            spread(blk)

    def relay(zz):
        blk = device(zz, 1 - y, c)
        block(blk, 2, across).wait_recv()
        block(blk, 3, sibling).start()

    relay(z)
    for d in range(1, Z):
        @pl.when(z - d >= 0)
        def _():
            relay(z - d)

        @pl.when(z + d < Z)
        def _():
            relay(z + d)

    for zz in range(Z):
        for yy in range(2):
            block(device(zz, yy, 1 - c), 3, sibling).wait_recv()

    @pl.loop(0, count // tile)
    def _(t):
        rows = pl.ds(pl.multiple_of(t * tile, tile), tile)
        projected = dot(points[rows, :], w[...].reshape(D, WIDTH))
        feat[rows, :] = projected[:, :D].astype(BF16)
        logits = projected[:, D:].T.reshape(H, M, tile)
        e = jnp.exp(logits - jnp.max(logits, axis=1, keepdims=True))
        s = (e / jnp.sum(e, axis=1, keepdims=True)).reshape(H * M, tile)
        soft[:, rows] = s
        softb[:, rows] = s.astype(BF16)

    ones = jnp.ones((8, count), BF16)
    for j in range(4):
        sl, fl = slice(128 * j, 128 * j + 128), slice(256 * j, 256 * j + 256)
        s = softb[sl, :]
        rf, rg = dot(s, feat[:, fl]), dot(s, cot[:, fl])
        mass = dot(ones, s, (1, 1))
        for hh in range(4):
            a, b = slice(32 * hh, 32 * hh + 32), slice(64 * hh, 64 * hh + 64)
            stat[4 * j + hh, 0:32, :] = jnp.concatenate([rf[a, b], rg[a, b]], axis=1)
            stat[4 * j + hh, 32:40, :] = mass

    def piece(to):
        return remote(stat.at[to], rbuf.at[me], ssend.at[0, to], srecv.at[0, me], to)

    def landed(k):
        return remote(stat.at[k], rbuf.at[k], ssend.at[0, k], srecv.at[0, k], k)

    @pl.loop(1, N)
    def _(k):
        piece(lax.rem(me + k, N)).start()

    rbuf[me] = stat[me]

    @pl.loop(1, N)
    def _(k):
        landed(lax.rem(me + k, N)).wait_recv()

    full[me] = jnp.sum(rbuf[...], axis=0)

    def total(to):
        return remote(full.at[me], full.at[me], ssend.at[1, to], srecv.at[1, me], to)

    def total_landed(k):
        return remote(full.at[k], full.at[k], ssend.at[1, k], srecv.at[1, k], k)

    @pl.loop(1, N)
    def _(k):
        total(lax.rem(me + k, N)).start()

    @pl.loop(1, N)
    def _(k):
        total_landed(lax.rem(me + k, N)).wait_recv()

    wq, wk, wv = tw[0], tw[1], tw[2]
    row_head = lax.broadcasted_iota(jnp.int32, (128, 128), 0) // M
    col_head = lax.broadcasted_iota(jnp.int32, (128, 128), 1) // M
    same = row_head == col_head
    wide = (
        lax.broadcasted_iota(jnp.int32, (128, 256), 0) // M
        == lax.broadcasted_iota(jnp.int32, (128, 256), 1) // DH
    )
    gq = gk = gv = jnp.zeros((DH, DH), F32)
    for j in range(4):
        sums = full[4 * j : 4 * j + 4, 0:32, 0:64].reshape(128, DH)
        d_mixed = full[4 * j : 4 * j + 4, 0:32, 64:128].reshape(128, DH)
        denom = jnp.broadcast_to(full[4 * j, 32:33, :], (128, 128)).T[:, :DH] + 1e-05
        tokens = sums / denom
        q = dot(tokens, wq, precision=HIGHEST)
        k = dot(tokens, wk, precision=HIGHEST)
        v = dot(tokens, wv, precision=HIGHEST)
        scores = dot(q, k, (1, 1), HIGHEST) * 0.125
        scores = jnp.where(same, scores, -jnp.inf)
        e = jnp.exp(scores - jnp.max(scores, axis=1, keepdims=True))
        attend = e / jnp.sum(e, axis=1, keepdims=True)
        mixed = dot(attend, v, precision=HIGHEST)
        d_attend = dot(d_mixed, v, (1, 1), HIGHEST)
        dv = dot(attend, d_mixed, (0, 0), HIGHEST)
        d_attend = jnp.where(same, d_attend, 0.0)
        ds = attend * (d_attend - jnp.sum(attend * d_attend, axis=1, keepdims=True)) * 0.125
        dq = dot(ds, k, precision=HIGHEST)
        dk = dot(ds, q, (0, 0), HIGHEST)
        d_tokens = (
            dot(dq, wq, (1, 1), HIGHEST)
            + dot(dk, wk, (1, 1), HIGHEST)
            + dot(dv, wv, (1, 1), HIGHEST)
        )
        gq += dot(tokens, dq, (0, 0), HIGHEST)
        gk += dot(tokens, dk, (0, 0), HIGHEST)
        gv += dot(tokens, dv, (0, 0), HIGHEST)
        d_sums = d_tokens / denom
        d_mass = -jnp.sum(d_tokens * tokens, axis=1, keepdims=True) / denom[:, 0:1]
        sl = slice(128 * j, 128 * j + 128)
        mix_m[sl, :] = jnp.where(wide, jnp.concatenate([mixed] * 4, axis=1), 0.0).astype(BF16)
        dsum_m[sl, :] = jnp.where(wide, jnp.concatenate([d_sums] * 4, axis=1), 0.0).astype(BF16)
        dmass[sl, :] = jnp.broadcast_to(d_mass, (128, 128))
    gtw[0] = gq
    gtw[1] = gk
    gtw[2] = gv

    for j in range(4):
        sl, fl = slice(128 * j, 128 * j + 128), slice(256 * j, 256 * j + 256)
        d_soft = (
            dot(mix_m[sl, :], cot[:, fl], (1, 1))
            + dot(dsum_m[sl, :], feat[:, fl], (1, 1))
            + dmass[sl, 0:1]
        )
        s = soft[sl, :]
        inner = jnp.sum((s * d_soft).reshape(4, M, count), axis=1, keepdims=True)
        d_logits = s.reshape(4, M, count) * (d_soft.reshape(4, M, count) - inner)
        grads[:, D + 128 * j : D + 128 * j + 128] = d_logits.reshape(128, count).T.astype(BF16)
        grads[:, fl] = dot(softb[sl, :], dsum_m[sl, :], (0, 0)).astype(BF16)

    def to_core(u):
        return remote(cbuf.at[u], crbuf.at[u], csend.at[u], crecv.at[u], sibling)

    def to_across(u):
        return remote(ybuf.at[u], yrbuf.at[u], ysend.at[u], yrecv.at[u], across)

    def to_owner(u):
        return remote(
            zbuf.at[u], zrbuf.at[u], zsend.at[u], zrecv.at[u],
            device(lax.rem(z + 1 + u, Z), y, c),
        )

    unit = 4 * ROWS

    @pl.loop(0, Z)
    def _(u):
        zz = lax.rem(z + 1 + u, Z)
        rows = pl.ds(pl.multiple_of(zz * unit, unit), unit)
        part[u] = dot(pts_t[rows, :], grads[...])
        for yy in range(2):
            other = pl.ds(pl.multiple_of(yy * 2 * ROWS + (1 - c) * ROWS, ROWS), ROWS)
            cbuf[u, yy] = part[u, other, :].astype(BF16)
        to_core(u).start()

    @pl.loop(0, Z)
    def _(u):
        to_core(u).wait_recv()
        theirs = pl.ds(pl.multiple_of((1 - y) * 2 * ROWS + c * ROWS, ROWS), ROWS)
        mine = pl.ds(pl.multiple_of(y * 2 * ROWS + c * ROWS, ROWS), ROWS)
        ybuf[u] = (part[u, theirs, :] + crbuf[u, 1 - y].astype(F32)).astype(BF16)
        to_across(u).start()
        keep[u] = part[u, mine, :] + crbuf[u, y].astype(F32)

    @pl.loop(0, count // tile)
    def _(t):
        rows = pl.ds(pl.multiple_of(t * tile, tile), tile)
        gp[rows, :] = dot(grads[rows, :], w[...].reshape(D, WIDTH), (1, 1)).astype(BF16)

    @pl.loop(0, Z - 1)
    def _(u):
        to_across(u).wait_recv()
        zbuf[u] = (keep[u] + yrbuf[u].astype(F32)).astype(BF16)
        to_owner(u).start()

    to_across(Z - 1).wait_recv()
    own = keep[Z - 1] + yrbuf[Z - 1].astype(F32)
    for u in range(Z - 1):
        to_owner(u).wait_recv()
        own = own + zrbuf[u].astype(F32)
    gw[...] = own

    for zz in range(Z):
        block(device(zz, y, c), 2, across).wait_send()
        for yy in range(2):
            block(device(zz, yy, c), 3, sibling).wait_send()

        @pl.when((z < Z - 1) & (zz <= z))
        def _():
            block(device(zz, y, c), 0, to_up).wait_send()

        @pl.when((z > 0) & (zz >= z))
        def _():
            block(device(zz, y, c), 1, to_down).wait_send()

    @pl.loop(1, N)
    def _(k):
        piece(lax.rem(me + k, N)).wait_send()
        total(lax.rem(me + k, N)).wait_send()

    @pl.loop(0, Z)
    def _(u):
        to_core(u).wait_send()
        to_across(u).wait_send()

    @pl.loop(0, Z - 1)
    def _(u):
        to_owner(u).wait_send()


def fused(points, in_weight, slice_token_weight, cotangent):
    count = points.shape[0]
    vmem = pl.BlockSpec(memory_space=pltpu.VMEM)
    dma = pltpu.SemaphoreType.DMA
    return pl.pallas_call(
        kernel,
        out_shape=(
            jax.ShapeDtypeStruct((count, D), BF16),
            jax.ShapeDtypeStruct((ROWS, WIDTH), F32),
            jax.ShapeDtypeStruct((3, DH, DH), F32),
        ),
        in_specs=[vmem] * 4,
        out_specs=(vmem,) * 3,
        scratch_shapes=[
            pltpu.VMEM((N, ROWS, WIDTH), BF16),
            pltpu.VMEM((D, count), BF16),
            pltpu.VMEM((count, D), BF16),
            pltpu.VMEM((H * M, count), F32),
            pltpu.VMEM((H * M, count), BF16),
            pltpu.VMEM((N, 40, 128), F32),
            pltpu.VMEM((N, 40, 128), F32),
            pltpu.VMEM((N, 40, 128), F32),
            pltpu.VMEM((H * M, 256), BF16),
            pltpu.VMEM((H * M, 256), BF16),
            pltpu.VMEM((H * M, 128), F32),
            pltpu.VMEM((count, WIDTH), BF16),
            pltpu.VMEM((Z, 4 * ROWS, WIDTH), F32),
            pltpu.VMEM((Z, ROWS, WIDTH), F32),
            pltpu.VMEM((Z, 2, ROWS, WIDTH), BF16),
            pltpu.VMEM((Z, 2, ROWS, WIDTH), BF16),
            pltpu.VMEM((Z, ROWS, WIDTH), BF16),
            pltpu.VMEM((Z, ROWS, WIDTH), BF16),
            pltpu.VMEM((Z - 1, ROWS, WIDTH), BF16),
            pltpu.VMEM((Z - 1, ROWS, WIDTH), BF16),
            dma((4, N)), dma((N,)), dma((2, N)), dma((2, N)),
            dma((Z,)), dma((Z,)), dma((Z,)), dma((Z,)), dma((Z - 1,)), dma((Z - 1,)),
        ],
        compiler_params=pltpu.CompilerParams(
            collective_id=0, has_side_effects=True, vmem_limit_bytes=60 * 1024 * 1024
        ),
    )(points, in_weight, slice_token_weight, cotangent)


def solution(mesh):
    body = fused if mesh.shape["seq"] == N else local

    return jax.shard_map(
        body,
        mesh=mesh,
        in_specs=(P(("groups", "seq"), None), P("seq", None), P(), P(("groups", "seq"), None)),
        out_specs=(P(("groups", "seq"), None), P(("groups", "seq"), None), P("groups", None, None)),
        check_vma=False,
    )
```

```python
import jax
import jax.numpy as jnp
from jax import lax
from jax.experimental import pallas as pl
from jax.experimental.pallas import tpu as pltpu
from jax.sharding import PartitionSpec as P

D = 1024
H = 16
M = 32
DH = 64


def token_mixing(slice_tokens, slice_token_weight):
    highest_precision = lax.Precision.HIGHEST
    query_rows = jnp.einsum(
        "pat,tg->pag", slice_tokens, slice_token_weight[0], precision=highest_precision
    )
    key_matrix = jnp.einsum(
        "pat,tg->pag", slice_tokens, slice_token_weight[1], precision=highest_precision
    )
    value_matrix = jnp.einsum(
        "pat,tg->pag", slice_tokens, slice_token_weight[2], precision=highest_precision
    )
    scores = jnp.einsum(
        "hme,hke->hmk", query_rows, key_matrix, precision=highest_precision
    ) / jnp.sqrt(jnp.float32(DH))
    attend = jax.nn.softmax(scores, axis=-1)
    return jnp.einsum("hmk,hke->hme", attend, value_matrix, precision=highest_precision)


def local(points, in_weight, slice_token_weight, cotangent):
    count = points.shape[0]
    whole_weight = lax.all_gather(in_weight, "seq", axis=0, tiled=True)
    projected = jnp.dot(points, whole_weight, preferred_element_type=jnp.float32)
    point_features = projected[:, :D].astype(jnp.bfloat16).reshape(count, H, DH)
    soft = jax.nn.softmax(projected[:, D:].reshape(count, H, M), axis=-1)
    backward_softmax = soft.astype(jnp.bfloat16)
    backward_gradient = cotangent.reshape(count, H, DH)
    mass = jnp.sum(backward_softmax.astype(jnp.float32), axis=0)
    slice_totals = jnp.einsum(
        "uog,uoa->oga", backward_softmax, point_features, preferred_element_type=jnp.float32
    )
    mass, slice_totals = lax.psum((mass, slice_totals), "seq")
    denom = mass + 1e-05
    slice_tokens = slice_totals / denom[:, :, None]
    mixed, mix_vjp = jax.vjp(token_mixing, slice_tokens, slice_token_weight)
    backward_mixed_tokens = mixed.astype(jnp.bfloat16)
    local_mixed_tokens = jnp.einsum(
        "uog,uoa->oga", backward_softmax, backward_gradient, preferred_element_type=jnp.float32
    )
    mixed_tokens_gradient = lax.psum(local_mixed_tokens, "seq")
    d_tokens, grad_token_weights = mix_vjp(mixed_tokens_gradient)
    slice_totals_gradient = (d_tokens / denom[:, :, None]).astype(jnp.bfloat16)
    slice_mass_gradient = -jnp.sum(d_tokens * slice_tokens, axis=-1) / denom
    softmax_gradient = jnp.einsum(
        "ugv,gfv->ugf", backward_gradient, backward_mixed_tokens, preferred_element_type=jnp.float32
    )
    softmax_gradient = (
        softmax_gradient
        + jnp.einsum(
            "ugv,gfv->ugf",
            point_features,
            slice_totals_gradient,
            preferred_element_type=jnp.float32,
        )
        + slice_mass_gradient[None]
    )
    d_logits = soft * (softmax_gradient - jnp.sum(soft * softmax_gradient, axis=-1, keepdims=True))
    feature_gradient = jnp.einsum(
        "lvt,vtz->lvz", backward_softmax, slice_totals_gradient, preferred_element_type=jnp.float32
    )
    grads = jnp.concatenate(
        [feature_gradient.reshape(count, D), d_logits.reshape(count, H * M)], axis=1
    ).astype(jnp.bfloat16)
    back = lax.dot_general(
        grads, whole_weight, (((1,), (1,)), ((), ())), preferred_element_type=jnp.float32
    )
    grad_points = back.astype(jnp.bfloat16)
    grad_in_weight = lax.psum_scatter(
        lax.dot_general(
            points, grads, (((0,), (0,)), ((), ())), preferred_element_type=jnp.float32
        ),
        "seq",
        scatter_dimension=0,
        tiled=True,
    )
    return (grad_points, grad_in_weight, grad_token_weights)


MESH = pl.DeviceIdType.MESH
F32 = jnp.float32
BF16 = jnp.bfloat16
HIGHEST = lax.Precision.HIGHEST
N = 16
Z = 4
ROWS = D // N
WIDTH = D + H * M


def dot(a, b, dims=(1, 0), precision=None):
    return lax.dot_general(
        a, b, (((dims[0],), (dims[1],)), ((), ())), precision=precision, preferred_element_type=F32
    )


def kernel(
    points_hbm, win, tw, cot_hbm, gp_hbm, gw, gtw,
    points, cot, gp, w, pts_t, feat, soft, softb, stat, rbuf, full, dsum_m, mix_m, dmass, grads,
    part, keep, cbuf, crbuf, ybuf, yrbuf, zbuf, zrbuf,
    load, store, gsend, grecv, ssend, srecv, csend, crecv, ysend, yrecv, zsend, zrecv,
):
    count = points.shape[0]
    tile = 256
    me = lax.axis_index("seq")
    z, y, c = me // 4, (me // 2) % 2, me % 2

    def device(zz, yy, cc):
        return (zz * 2 + yy) * 2 + cc

    sibling, across = device(z, y, 1 - c), device(z, 1 - y, c)

    def remote(src, dst, send, recv, to):
        return pltpu.make_async_remote_copy(
            src_ref=src, dst_ref=dst, send_sem=send, recv_sem=recv,
            device_id={"seq": to}, device_id_type=MESH,
        )

    barrier = pltpu.get_barrier_semaphore()

    @pl.loop(1, N)
    def _(k):
        pl.semaphore_signal(
            barrier, inc=1, device_id={"seq": lax.rem(me + k, N)}, device_id_type=MESH
        )

    loads = [
        pltpu.make_async_copy(win, w.at[me], load.at[0]),
        pltpu.make_async_copy(points_hbm, points, load.at[1]),
        pltpu.make_async_copy(cot_hbm, cot, load.at[2]),
    ]
    for copy in loads:
        copy.start()
    loads[0].wait()
    pl.semaphore_wait(barrier, N - 1)

    def block(blk, slot, to):
        return remote(w.at[blk], w.at[blk], gsend.at[slot, blk], grecv.at[blk], to)

    up = jnp.minimum(z + 1, Z - 1)
    down = jnp.maximum(z - 1, 0)
    to_up, to_down = device(up, y, c), device(down, y, c)

    def spread(blk):
        block(blk, 2, across).start()
        block(blk, 3, sibling).start()

    @pl.when(z < Z - 1)
    def _():
        block(me, 0, to_up).start()

    @pl.when(z > 0)
    def _():
        block(me, 1, to_down).start()

    spread(me)

    loads[1].wait()
    for k in range(D // tile):
        cols = slice(k * tile, (k + 1) * tile)
        pts_t[cols, :] = points[:, cols].T

    def partner(mask):
        return 2 * lax.rem(z // 2 + mask // 2, 2) + lax.rem(z + mask, 2)

    def forward(d):
        @pl.when(z - d >= 0)
        def _():
            blk = device(z - d, y, c)
            block(blk, 0, to_up).wait_recv()

            @pl.when(z < Z - 1)
            def _():
                block(blk, 0, to_up).start()

            spread(blk)

        @pl.when(z + d < Z)
        def _():
            blk = device(z + d, y, c)
            block(blk, 1, to_down).wait_recv()

            @pl.when(z > 0)
            def _():
                block(blk, 1, to_down).start()

            spread(blk)

    def plane_arrives(zz):
        blk = device(zz, 1 - y, c)
        block(blk, 2, across).wait_recv()
        block(blk, 3, sibling).start()
        for yy in range(2):
            block(device(zz, yy, 1 - c), 3, sibling).wait_recv()

    def plane_term(zz, rows):
        cols = pl.ds(pl.multiple_of(zz * 4 * ROWS, 4 * ROWS), 4 * ROWS)
        return dot(points[rows, cols], w[pl.ds(4 * zz, 4)].reshape(4 * ROWS, WIDTH))

    @pl.loop(0, Z - 1)
    def _(step):
        forward(step + 1)
        zz = partner(step)
        plane_arrives(zz)

        @pl.loop(0, count // tile)
        def _(t):
            term = plane_term(zz, pl.ds(pl.multiple_of(t * tile, tile), tile))

            @pl.when(step == 0)
            def _():
                part[t] = term

            @pl.when(step > 0)
            def _():
                part[t] += term

    plane_arrives(partner(Z - 1))
    loads[2].wait()

    @pl.loop(0, count // tile)
    def _(t):
        rows = pl.ds(pl.multiple_of(t * tile, tile), tile)
        projected = part[t] + plane_term(partner(Z - 1), rows)
        feat[rows, :] = projected[:, :D].astype(BF16)
        logits = projected[:, D:].T.reshape(H, M, tile)
        e = jnp.exp(logits - jnp.max(logits, axis=1, keepdims=True))
        s = (e / jnp.sum(e, axis=1, keepdims=True)).reshape(H * M, tile)
        soft[:, rows] = s
        softb[:, rows] = s.astype(BF16)

    ones = jnp.ones((8, count), BF16)
    for j in range(4):
        sl, fl = slice(128 * j, 128 * j + 128), slice(256 * j, 256 * j + 256)
        s = softb[sl, :]
        rf, rg = dot(s, feat[:, fl]), dot(s, cot[:, fl])
        mass = dot(ones, s, (1, 1))
        for hh in range(4):
            a, b = slice(32 * hh, 32 * hh + 32), slice(64 * hh, 64 * hh + 64)
            stat[4 * j + hh, 0:32, :] = jnp.concatenate([rf[a, b], rg[a, b]], axis=1)
            stat[4 * j + hh, 32:40, :] = mass

    def piece(to):
        return remote(stat.at[to], rbuf.at[me], ssend.at[0, to], srecv.at[0, me], to)

    def landed(k):
        return remote(stat.at[k], rbuf.at[k], ssend.at[0, k], srecv.at[0, k], k)

    @pl.loop(1, N)
    def _(k):
        piece(lax.rem(me + k, N)).start()

    rbuf[me] = stat[me]

    @pl.loop(1, N)
    def _(k):
        landed(lax.rem(me + k, N)).wait_recv()

    full[me] = jnp.sum(rbuf[...], axis=0)

    def total(to):
        return remote(full.at[me], full.at[me], ssend.at[1, to], srecv.at[1, me], to)

    def total_landed(k):
        return remote(full.at[k], full.at[k], ssend.at[1, k], srecv.at[1, k], k)

    @pl.loop(1, N)
    def _(k):
        total(lax.rem(me + k, N)).start()

    @pl.loop(1, N)
    def _(k):
        total_landed(lax.rem(me + k, N)).wait_recv()

    wq, wk, wv = tw[0], tw[1], tw[2]
    row_head = lax.broadcasted_iota(jnp.int32, (128, 128), 0) // M
    col_head = lax.broadcasted_iota(jnp.int32, (128, 128), 1) // M
    same = row_head == col_head
    wide = (
        lax.broadcasted_iota(jnp.int32, (128, 256), 0) // M
        == lax.broadcasted_iota(jnp.int32, (128, 256), 1) // DH
    )
    gq = gk = gv = jnp.zeros((DH, DH), F32)
    for j in range(4):
        sums = full[4 * j : 4 * j + 4, 0:32, 0:64].reshape(128, DH)
        d_mixed = full[4 * j : 4 * j + 4, 0:32, 64:128].reshape(128, DH)
        denom = jnp.broadcast_to(full[4 * j, 32:33, :], (128, 128)).T[:, :DH] + 1e-05
        tokens = sums / denom
        q = dot(tokens, wq, precision=HIGHEST)
        k = dot(tokens, wk, precision=HIGHEST)
        v = dot(tokens, wv, precision=HIGHEST)
        scores = dot(q, k, (1, 1), HIGHEST) * 0.125
        scores = jnp.where(same, scores, -jnp.inf)
        e = jnp.exp(scores - jnp.max(scores, axis=1, keepdims=True))
        attend = e / jnp.sum(e, axis=1, keepdims=True)
        mixed = dot(attend, v, precision=HIGHEST)
        d_attend = dot(d_mixed, v, (1, 1), HIGHEST)
        dv = dot(attend, d_mixed, (0, 0), HIGHEST)
        d_attend = jnp.where(same, d_attend, 0.0)
        ds = attend * (d_attend - jnp.sum(attend * d_attend, axis=1, keepdims=True)) * 0.125
        dq = dot(ds, k, precision=HIGHEST)
        dk = dot(ds, q, (0, 0), HIGHEST)
        d_tokens = (
            dot(dq, wq, (1, 1), HIGHEST)
            + dot(dk, wk, (1, 1), HIGHEST)
            + dot(dv, wv, (1, 1), HIGHEST)
        )
        gq += dot(tokens, dq, (0, 0), HIGHEST)
        gk += dot(tokens, dk, (0, 0), HIGHEST)
        gv += dot(tokens, dv, (0, 0), HIGHEST)
        d_sums = d_tokens / denom
        d_mass = -jnp.sum(d_tokens * tokens, axis=1, keepdims=True) / denom[:, 0:1]
        sl = slice(128 * j, 128 * j + 128)
        mix_m[sl, :] = jnp.where(wide, jnp.concatenate([mixed] * 4, axis=1), 0.0).astype(BF16)
        dsum_m[sl, :] = jnp.where(wide, jnp.concatenate([d_sums] * 4, axis=1), 0.0).astype(BF16)
        dmass[sl, :] = jnp.broadcast_to(d_mass, (128, 128))
    gtw[0] = gq
    gtw[1] = gk
    gtw[2] = gv

    for j in range(4):
        sl, fl = slice(128 * j, 128 * j + 128), slice(256 * j, 256 * j + 256)
        d_soft = (
            dot(mix_m[sl, :], cot[:, fl], (1, 1))
            + dot(dsum_m[sl, :], feat[:, fl], (1, 1))
            + dmass[sl, 0:1]
        )
        s = soft[sl, :]
        inner = jnp.sum((s * d_soft).reshape(4, M, count), axis=1, keepdims=True)
        d_logits = s.reshape(4, M, count) * (d_soft.reshape(4, M, count) - inner)
        grads[:, D + 128 * j : D + 128 * j + 128] = d_logits.reshape(128, count).T.astype(BF16)
        grads[:, fl] = dot(softb[sl, :], dsum_m[sl, :], (0, 0)).astype(BF16)

    def to_core(u):
        return remote(cbuf.at[u], crbuf.at[u], csend.at[u], crecv.at[u], sibling)

    def to_across(u):
        return remote(ybuf.at[u], yrbuf.at[u], ysend.at[u], yrecv.at[u], across)

    def unit_owner(u):
        return partner(Z - 1 - u)

    def to_owner(u):
        to = partner(2) if u == 1 else partner(1)
        return remote(
            zbuf.at[u], zrbuf.at[u], zsend.at[u], zrecv.at[u], device(to, y, c)
        )

    unit = 4 * ROWS

    def core_step(u):
        to_core(u).wait_recv()
        theirs = pl.ds(pl.multiple_of((1 - y) * 2 * ROWS + c * ROWS, ROWS), ROWS)
        mine = pl.ds(pl.multiple_of(y * 2 * ROWS + c * ROWS, ROWS), ROWS)
        ybuf[u] = (part[u, theirs, :] + crbuf[u, 1 - y].astype(F32)).astype(BF16)
        to_across(u).start()
        keep[u] = part[u, mine, :] + crbuf[u, y].astype(F32)

    @pl.loop(0, Z)
    def _(u):
        rows = pl.ds(pl.multiple_of(unit_owner(u) * unit, unit), unit)
        part[u] = dot(pts_t[rows, :], grads[...])
        for yy in range(2):
            other = pl.ds(pl.multiple_of(yy * 2 * ROWS + (1 - c) * ROWS, ROWS), ROWS)
            cbuf[u, yy] = part[u, other, :].astype(BF16)
        to_core(u).start()

        @pl.when(u > 0)
        def _():
            core_step(u - 1)

    core_step(Z - 1)

    def gp_copy(t):
        rows = pl.ds(pl.multiple_of(t * tile, tile), tile)
        return pltpu.make_async_copy(gp.at[rows, :], gp_hbm.at[rows, :], store.at[t])

    def gp_tiles(start, stop):
        @pl.loop(start, stop)
        def _(t):
            rows = pl.ds(pl.multiple_of(t * tile, tile), tile)
            gp[rows, :] = dot(grads[rows, :], w[...].reshape(D, WIDTH), (1, 1)).astype(BF16)
            gp_copy(t).start()

    def summed(u):
        to_across(u).wait_recv()
        return keep[u] + yrbuf[u].astype(F32)

    tiles = count // tile
    gp_tiles(0, tiles // 2)
    zbuf[0] = summed(0).astype(BF16)
    to_owner(0).start()
    gp_tiles(tiles // 2, tiles)
    second = summed(1)
    to_owner(0).wait_recv()
    zbuf[1] = (second + zrbuf[0].astype(F32)).astype(BF16)
    to_owner(1).start()
    zbuf[2] = summed(2).astype(BF16)
    to_owner(2).start()
    own = summed(3)
    to_owner(1).wait_recv()
    own = own + zrbuf[1].astype(F32)
    to_owner(2).wait_recv()
    gw[...] = own + zrbuf[2].astype(F32)

    @pl.loop(0, tiles)
    def _(t):
        gp_copy(t).wait()

    for zz in range(Z):
        block(device(zz, y, c), 2, across).wait_send()
        for yy in range(2):
            block(device(zz, yy, c), 3, sibling).wait_send()

        @pl.when((z < Z - 1) & (zz <= z))
        def _():
            block(device(zz, y, c), 0, to_up).wait_send()

        @pl.when((z > 0) & (zz >= z))
        def _():
            block(device(zz, y, c), 1, to_down).wait_send()

    @pl.loop(1, N)
    def _(k):
        piece(lax.rem(me + k, N)).wait_send()
        total(lax.rem(me + k, N)).wait_send()

    @pl.loop(0, Z)
    def _(u):
        to_core(u).wait_send()
        to_across(u).wait_send()

    for u in range(Z - 1):
        to_owner(u).wait_send()


def hand_on(*refs):
    n = (len(refs) - 1) // 2
    sems = refs[-1]
    copies = []
    for i in range(n):
        src, dst = refs[i], refs[n + i]
        pieces = 8 if i == 0 else 1
        size = src.shape[0] // pieces
        for k in range(pieces):
            rows = pl.ds(k * size, size)
            copies.append(
                pltpu.make_async_copy(src.at[rows], dst.at[rows], sems.at[len(copies)])
            )
    for copy in copies:
        copy.start()
    for copy in copies:
        copy.wait()


def fused(points, in_weight, slice_token_weight, cotangent):
    count = points.shape[0]
    vmem = pl.BlockSpec(memory_space=pltpu.VMEM)
    dma = pltpu.SemaphoreType.DMA
    hbm = pl.BlockSpec(memory_space=pl.ANY)
    out_shape = (
        jax.ShapeDtypeStruct((count, D), BF16),
        jax.ShapeDtypeStruct((ROWS, WIDTH), F32),
        jax.ShapeDtypeStruct((3, DH, DH), F32),
    )
    outs = pl.pallas_call(
        kernel,
        out_shape=out_shape,
        in_specs=[hbm, hbm, vmem, hbm],
        out_specs=(hbm, vmem, vmem),
        scratch_shapes=[
            pltpu.VMEM((count, D), BF16),
            pltpu.VMEM((count, D), BF16),
            pltpu.VMEM((count, D), BF16),
            pltpu.VMEM((N, ROWS, WIDTH), BF16),
            pltpu.VMEM((D, count), BF16),
            pltpu.VMEM((count, D), BF16),
            pltpu.VMEM((H * M, count), F32),
            pltpu.VMEM((H * M, count), BF16),
            pltpu.VMEM((N, 40, 128), F32),
            pltpu.VMEM((N, 40, 128), F32),
            pltpu.VMEM((N, 40, 128), F32),
            pltpu.VMEM((H * M, 256), BF16),
            pltpu.VMEM((H * M, 256), BF16),
            pltpu.VMEM((H * M, 128), F32),
            pltpu.VMEM((count, WIDTH), BF16),
            pltpu.VMEM((Z, 4 * ROWS, WIDTH), F32),
            pltpu.VMEM((Z, ROWS, WIDTH), F32),
            pltpu.VMEM((Z, 2, ROWS, WIDTH), BF16),
            pltpu.VMEM((Z, 2, ROWS, WIDTH), BF16),
            pltpu.VMEM((Z, ROWS, WIDTH), BF16),
            pltpu.VMEM((Z, ROWS, WIDTH), BF16),
            pltpu.VMEM((Z - 1, ROWS, WIDTH), BF16),
            pltpu.VMEM((Z - 1, ROWS, WIDTH), BF16),
            dma((3,)), dma((4,)), dma((4, N)), dma((N,)), dma((2, N)), dma((2, N)),
            dma((Z,)), dma((Z,)), dma((Z,)), dma((Z,)), dma((Z - 1,)), dma((Z - 1,)),
        ],
        compiler_params=pltpu.CompilerParams(
            collective_id=0, has_side_effects=True, vmem_limit_bytes=60 * 1024 * 1024
        ),
    )(points, in_weight, slice_token_weight, cotangent)
    return pl.pallas_call(
        hand_on,
        out_shape=out_shape,
        in_specs=[hbm] * 3,
        out_specs=(hbm,) * 3,
        scratch_shapes=[dma((10,))],
    )(*outs)


def solution(mesh):
    body = fused if mesh.shape["seq"] == N else local

    return jax.shard_map(
        body,
        mesh=mesh,
        in_specs=(P(("groups", "seq"), None), P("seq", None), P(), P(("groups", "seq"), None)),
        out_specs=(P(("groups", "seq"), None), P(("groups", "seq"), None), P("groups", None, None)),
        check_vma=False,
    )
```

```python
import jax
import jax.numpy as jnp
from jax import lax
from jax.experimental import pallas as pl
from jax.experimental.pallas import tpu as pltpu
from jax.sharding import PartitionSpec as P

D = 1024
H = 16
M = 32
DH = 64


def token_mixing(slice_tokens, slice_token_weight):
    highest_precision = lax.Precision.HIGHEST
    query_rows = jnp.einsum(
        "pat,tg->pag", slice_tokens, slice_token_weight[0], precision=highest_precision
    )
    key_matrix = jnp.einsum(
        "pat,tg->pag", slice_tokens, slice_token_weight[1], precision=highest_precision
    )
    value_matrix = jnp.einsum(
        "pat,tg->pag", slice_tokens, slice_token_weight[2], precision=highest_precision
    )
    scores = jnp.einsum(
        "hme,hke->hmk", query_rows, key_matrix, precision=highest_precision
    ) / jnp.sqrt(jnp.float32(DH))
    attend = jax.nn.softmax(scores, axis=-1)
    return jnp.einsum("hmk,hke->hme", attend, value_matrix, precision=highest_precision)


def local(points, in_weight, slice_token_weight, cotangent):
    count = points.shape[0]
    whole_weight = lax.all_gather(in_weight, "seq", axis=0, tiled=True)
    projected = jnp.dot(points, whole_weight, preferred_element_type=jnp.float32)
    point_features = projected[:, :D].astype(jnp.bfloat16).reshape(count, H, DH)
    soft = jax.nn.softmax(projected[:, D:].reshape(count, H, M), axis=-1)
    backward_softmax = soft.astype(jnp.bfloat16)
    backward_gradient = cotangent.reshape(count, H, DH)
    mass = jnp.sum(backward_softmax.astype(jnp.float32), axis=0)
    slice_totals = jnp.einsum(
        "uog,uoa->oga", backward_softmax, point_features, preferred_element_type=jnp.float32
    )
    mass, slice_totals = lax.psum((mass, slice_totals), "seq")
    denom = mass + 1e-05
    slice_tokens = slice_totals / denom[:, :, None]
    mixed, mix_vjp = jax.vjp(token_mixing, slice_tokens, slice_token_weight)
    backward_mixed_tokens = mixed.astype(jnp.bfloat16)
    local_mixed_tokens = jnp.einsum(
        "uog,uoa->oga", backward_softmax, backward_gradient, preferred_element_type=jnp.float32
    )
    mixed_tokens_gradient = lax.psum(local_mixed_tokens, "seq")
    d_tokens, grad_token_weights = mix_vjp(mixed_tokens_gradient)
    slice_totals_gradient = (d_tokens / denom[:, :, None]).astype(jnp.bfloat16)
    slice_mass_gradient = -jnp.sum(d_tokens * slice_tokens, axis=-1) / denom
    softmax_gradient = jnp.einsum(
        "ugv,gfv->ugf", backward_gradient, backward_mixed_tokens, preferred_element_type=jnp.float32
    )
    softmax_gradient = (
        softmax_gradient
        + jnp.einsum(
            "ugv,gfv->ugf",
            point_features,
            slice_totals_gradient,
            preferred_element_type=jnp.float32,
        )
        + slice_mass_gradient[None]
    )
    d_logits = soft * (softmax_gradient - jnp.sum(soft * softmax_gradient, axis=-1, keepdims=True))
    feature_gradient = jnp.einsum(
        "lvt,vtz->lvz", backward_softmax, slice_totals_gradient, preferred_element_type=jnp.float32
    )
    grads = jnp.concatenate(
        [feature_gradient.reshape(count, D), d_logits.reshape(count, H * M)], axis=1
    ).astype(jnp.bfloat16)
    back = lax.dot_general(
        grads, whole_weight, (((1,), (1,)), ((), ())), preferred_element_type=jnp.float32
    )
    grad_points = back.astype(jnp.bfloat16)
    grad_in_weight = lax.psum_scatter(
        lax.dot_general(
            points, grads, (((0,), (0,)), ((), ())), preferred_element_type=jnp.float32
        ),
        "seq",
        scatter_dimension=0,
        tiled=True,
    )
    return (grad_points, grad_in_weight, grad_token_weights)


MESH = pl.DeviceIdType.MESH
F32 = jnp.float32
BF16 = jnp.bfloat16
HIGHEST = lax.Precision.HIGHEST
N = 16
Z = 4
ROWS = D // N
WIDTH = D + H * M


def dot(a, b, dims=(1, 0), precision=None):
    return lax.dot_general(
        a, b, (((dims[0],), (dims[1],)), ((), ())), precision=precision, preferred_element_type=F32
    )


def kernel(
    points_hbm, win, tw, cot_hbm, gp_hbm, gw, gtw,
    points, cot, gp, w, pts_t, feat, soft, softb, stat, rbuf, full, dsum_m, mix_m, dmass, grads,
    part, keep, cbuf, crbuf, ybuf, yrbuf, zbuf, zrbuf,
    load, store, gsend, grecv, ssend, srecv, csend, crecv, ysend, yrecv, zsend, zrecv,
):
    count = points.shape[0]
    tile = 256
    me = lax.axis_index("seq")
    z, y, c = me // 4, (me // 2) % 2, me % 2

    def device(zz, yy, cc):
        return (zz * 2 + yy) * 2 + cc

    sibling, across = device(z, y, 1 - c), device(z, 1 - y, c)

    def remote(src, dst, send, recv, to):
        return pltpu.make_async_remote_copy(
            src_ref=src, dst_ref=dst, send_sem=send, recv_sem=recv,
            device_id={"seq": to}, device_id_type=MESH,
        )

    barrier = pltpu.get_barrier_semaphore()

    @pl.loop(1, N)
    def _(k):
        pl.semaphore_signal(
            barrier, inc=1, device_id={"seq": lax.rem(me + k, N)}, device_id_type=MESH
        )

    loads = [
        pltpu.make_async_copy(win, w.at[me], load.at[0]),
        pltpu.make_async_copy(points_hbm, points, load.at[1]),
        pltpu.make_async_copy(cot_hbm, cot, load.at[2]),
    ]
    for copy in loads:
        copy.start()
    loads[0].wait()
    pl.semaphore_wait(barrier, N - 1)

    def block(blk, slot, to):
        return remote(w.at[blk], w.at[blk], gsend.at[slot, blk], grecv.at[blk], to)

    up = jnp.minimum(z + 1, Z - 1)
    down = jnp.maximum(z - 1, 0)
    to_up, to_down = device(up, y, c), device(down, y, c)

    def spread(blk):
        block(blk, 2, across).start()
        block(blk, 3, sibling).start()

    @pl.when(z < Z - 1)
    def _():
        block(me, 0, to_up).start()

    @pl.when(z > 0)
    def _():
        block(me, 1, to_down).start()

    spread(me)

    loads[1].wait()
    for k in range(D // tile):
        cols = slice(k * tile, (k + 1) * tile)
        pts_t[cols, :] = points[:, cols].T

    def partner(mask):
        return 2 * lax.rem(z // 2 + mask // 2, 2) + lax.rem(z + mask, 2)

    def forward(d):
        @pl.when(z - d >= 0)
        def _():
            blk = device(z - d, y, c)
            block(blk, 0, to_up).wait_recv()

            @pl.when(z < Z - 1)
            def _():
                block(blk, 0, to_up).start()

            spread(blk)

        @pl.when(z + d < Z)
        def _():
            blk = device(z + d, y, c)
            block(blk, 1, to_down).wait_recv()

            @pl.when(z > 0)
            def _():
                block(blk, 1, to_down).start()

            spread(blk)

    def plane_arrives(zz):
        blk = device(zz, 1 - y, c)
        block(blk, 2, across).wait_recv()
        block(blk, 3, sibling).start()
        for yy in range(2):
            block(device(zz, yy, 1 - c), 3, sibling).wait_recv()

    def plane_term(zz, rows):
        cols = pl.ds(pl.multiple_of(zz * 4 * ROWS, 4 * ROWS), 4 * ROWS)
        return dot(points[rows, cols], w[pl.ds(4 * zz, 4)].reshape(4 * ROWS, WIDTH))

    @pl.loop(0, Z - 1)
    def _(step):
        forward(step + 1)
        zz = partner(step)
        plane_arrives(zz)

        @pl.loop(0, count // tile)
        def _(t):
            term = plane_term(zz, pl.ds(pl.multiple_of(t * tile, tile), tile))

            @pl.when(step == 0)
            def _():
                part[t] = term

            @pl.when(step > 0)
            def _():
                part[t] += term

    plane_arrives(partner(Z - 1))
    loads[2].wait()

    @pl.loop(0, count // tile)
    def _(t):
        rows = pl.ds(pl.multiple_of(t * tile, tile), tile)
        projected = part[t] + plane_term(partner(Z - 1), rows)
        feat[rows, :] = projected[:, :D].astype(BF16)
        logits = projected[:, D:].T.reshape(H, M, tile)
        e = jnp.exp(logits - jnp.max(logits, axis=1, keepdims=True))
        s = (e / jnp.sum(e, axis=1, keepdims=True)).reshape(H * M, tile)
        soft[:, rows] = s
        softb[:, rows] = s.astype(BF16)

    ones = jnp.ones((8, count), BF16)
    for j in range(4):
        sl, fl = slice(128 * j, 128 * j + 128), slice(256 * j, 256 * j + 256)
        s = softb[sl, :]
        rf, rg = dot(s, feat[:, fl]), dot(s, cot[:, fl])
        mass = dot(ones, s, (1, 1))
        for hh in range(4):
            a, b = slice(32 * hh, 32 * hh + 32), slice(64 * hh, 64 * hh + 64)
            stat[4 * j + hh, 0:32, :] = jnp.concatenate([rf[a, b], rg[a, b]], axis=1)
            stat[4 * j + hh, 32:40, :] = mass

    def piece(to):
        return remote(stat.at[to], rbuf.at[me], ssend.at[0, to], srecv.at[0, me], to)

    def landed(k):
        return remote(stat.at[k], rbuf.at[k], ssend.at[0, k], srecv.at[0, k], k)

    @pl.loop(1, N)
    def _(k):
        piece(lax.rem(me + k, N)).start()

    rbuf[me] = stat[me]

    @pl.loop(1, N)
    def _(k):
        landed(lax.rem(me + k, N)).wait_recv()

    full[me] = jnp.sum(rbuf[...], axis=0)

    def total(to):
        return remote(full.at[me], full.at[me], ssend.at[1, to], srecv.at[1, me], to)

    def total_landed(k):
        return remote(full.at[k], full.at[k], ssend.at[1, k], srecv.at[1, k], k)

    @pl.loop(1, N)
    def _(k):
        total(lax.rem(me + k, N)).start()

    @pl.loop(1, N)
    def _(k):
        total_landed(lax.rem(me + k, N)).wait_recv()

    wq, wk, wv = tw[0], tw[1], tw[2]
    row_head = lax.broadcasted_iota(jnp.int32, (128, 128), 0) // M
    col_head = lax.broadcasted_iota(jnp.int32, (128, 128), 1) // M
    same = row_head == col_head
    wide = (
        lax.broadcasted_iota(jnp.int32, (128, 256), 0) // M
        == lax.broadcasted_iota(jnp.int32, (128, 256), 1) // DH
    )
    gq = gk = gv = jnp.zeros((DH, DH), F32)
    for j in range(4):
        sums = full[4 * j : 4 * j + 4, 0:32, 0:64].reshape(128, DH)
        d_mixed = full[4 * j : 4 * j + 4, 0:32, 64:128].reshape(128, DH)
        denom = jnp.broadcast_to(full[4 * j, 32:33, :], (128, 128)).T[:, :DH] + 1e-05
        tokens = sums / denom
        q = dot(tokens, wq, precision=HIGHEST)
        k = dot(tokens, wk, precision=HIGHEST)
        v = dot(tokens, wv, precision=HIGHEST)
        scores = dot(q, k, (1, 1), HIGHEST) * 0.125
        scores = jnp.where(same, scores, -jnp.inf)
        e = jnp.exp(scores - jnp.max(scores, axis=1, keepdims=True))
        attend = e / jnp.sum(e, axis=1, keepdims=True)
        mixed = dot(attend, v, precision=HIGHEST)
        d_attend = dot(d_mixed, v, (1, 1), HIGHEST)
        dv = dot(attend, d_mixed, (0, 0), HIGHEST)
        d_attend = jnp.where(same, d_attend, 0.0)
        ds = attend * (d_attend - jnp.sum(attend * d_attend, axis=1, keepdims=True)) * 0.125
        dq = dot(ds, k, precision=HIGHEST)
        dk = dot(ds, q, (0, 0), HIGHEST)
        d_tokens = (
            dot(dq, wq, (1, 1), HIGHEST)
            + dot(dk, wk, (1, 1), HIGHEST)
            + dot(dv, wv, (1, 1), HIGHEST)
        )
        gq += dot(tokens, dq, (0, 0), HIGHEST)
        gk += dot(tokens, dk, (0, 0), HIGHEST)
        gv += dot(tokens, dv, (0, 0), HIGHEST)
        d_sums = d_tokens / denom
        d_mass = -jnp.sum(d_tokens * tokens, axis=1, keepdims=True) / denom[:, 0:1]
        sl = slice(128 * j, 128 * j + 128)
        mix_m[sl, :] = jnp.where(wide, jnp.concatenate([mixed] * 4, axis=1), 0.0).astype(BF16)
        dsum_m[sl, :] = jnp.where(wide, jnp.concatenate([d_sums] * 4, axis=1), 0.0).astype(BF16)
        dmass[sl, :] = jnp.broadcast_to(d_mass, (128, 128))
    gtw[0] = gq
    gtw[1] = gk
    gtw[2] = gv

    for j in range(4):
        sl, fl = slice(128 * j, 128 * j + 128), slice(256 * j, 256 * j + 256)
        d_soft = (
            dot(mix_m[sl, :], cot[:, fl], (1, 1))
            + dot(dsum_m[sl, :], feat[:, fl], (1, 1))
            + dmass[sl, 0:1]
        )
        s = soft[sl, :]
        inner = jnp.sum((s * d_soft).reshape(4, M, count), axis=1, keepdims=True)
        d_logits = s.reshape(4, M, count) * (d_soft.reshape(4, M, count) - inner)
        grads[:, D + 128 * j : D + 128 * j + 128] = d_logits.reshape(128, count).T.astype(BF16)
        grads[:, fl] = dot(softb[sl, :], dsum_m[sl, :], (0, 0)).astype(BF16)

    def to_core(u):
        return remote(cbuf.at[u], crbuf.at[u], csend.at[u], crecv.at[u], sibling)

    def to_across(u):
        return remote(ybuf.at[u], yrbuf.at[u], ysend.at[u], yrecv.at[u], across)

    def unit_owner(u):
        return partner(Z - 1 - u)

    def to_owner(u):
        to = partner(2) if u == 1 else partner(1)
        return remote(
            zbuf.at[u], zrbuf.at[u], zsend.at[u], zrecv.at[u], device(to, y, c)
        )

    unit = 4 * ROWS

    def core_step(u):
        to_core(u).wait_recv()
        theirs = pl.ds(pl.multiple_of((1 - y) * 2 * ROWS + c * ROWS, ROWS), ROWS)
        mine = pl.ds(pl.multiple_of(y * 2 * ROWS + c * ROWS, ROWS), ROWS)
        ybuf[u] = (part[u, theirs, :] + crbuf[u, 1 - y].astype(F32)).astype(BF16)
        to_across(u).start()
        keep[u] = part[u, mine, :] + crbuf[u, y].astype(F32)

    @pl.loop(0, Z)
    def _(u):
        rows = pl.ds(pl.multiple_of(unit_owner(u) * unit, unit), unit)
        part[u] = dot(pts_t[rows, :], grads[...])
        for yy in range(2):
            other = pl.ds(pl.multiple_of(yy * 2 * ROWS + (1 - c) * ROWS, ROWS), ROWS)
            cbuf[u, yy] = part[u, other, :].astype(BF16)
        to_core(u).start()

        @pl.when(u > 0)
        def _():
            core_step(u - 1)

    core_step(Z - 1)

    def gp_copy(t):
        rows = pl.ds(pl.multiple_of(t * tile, tile), tile)
        return pltpu.make_async_copy(gp.at[rows, :], gp_hbm.at[rows, :], store.at[t])

    def gp_tiles(start, stop):
        @pl.loop(start, stop)
        def _(t):
            rows = pl.ds(pl.multiple_of(t * tile, tile), tile)
            gp[rows, :] = dot(grads[rows, :], w[...].reshape(D, WIDTH), (1, 1)).astype(BF16)
            gp_copy(t).start()

    def summed(u):
        to_across(u).wait_recv()
        return keep[u] + yrbuf[u].astype(F32)

    tiles = count // tile
    gp_tiles(0, tiles // 2)
    zbuf[0] = summed(0).astype(BF16)
    to_owner(0).start()
    gp_tiles(tiles // 2, tiles)
    second = summed(1)
    to_owner(0).wait_recv()
    zbuf[1] = (second + zrbuf[0].astype(F32)).astype(BF16)
    to_owner(1).start()
    zbuf[2] = summed(2).astype(BF16)
    to_owner(2).start()
    own = summed(3)
    to_owner(1).wait_recv()
    own = own + zrbuf[1].astype(F32)
    to_owner(2).wait_recv()
    gw[...] = own + zrbuf[2].astype(F32)

    @pl.loop(0, tiles)
    def _(t):
        gp_copy(t).wait()

    for zz in range(Z):
        block(device(zz, y, c), 2, across).wait_send()
        for yy in range(2):
            block(device(zz, yy, c), 3, sibling).wait_send()

        @pl.when((z < Z - 1) & (zz <= z))
        def _():
            block(device(zz, y, c), 0, to_up).wait_send()

        @pl.when((z > 0) & (zz >= z))
        def _():
            block(device(zz, y, c), 1, to_down).wait_send()

    @pl.loop(1, N)
    def _(k):
        piece(lax.rem(me + k, N)).wait_send()
        total(lax.rem(me + k, N)).wait_send()

    @pl.loop(0, Z)
    def _(u):
        to_core(u).wait_send()
        to_across(u).wait_send()

    for u in range(Z - 1):
        to_owner(u).wait_send()


def hand_on(gp, gw, gtw, gp_out, gw_out, gtw_out, gp_v, gw_v, gtw_v, load, store):
    size = gp.shape[0] // 4
    steps = [
        (gp.at[pl.ds(k * size, size)], gp_v.at[pl.ds(k * size, size)], gp_out.at[pl.ds(k * size, size)])
        for k in range(4)
    ]
    steps += [(gw, gw_v, gw_out), (gtw, gtw_v, gtw_out)]
    loads = [pltpu.make_async_copy(a, b, load.at[i]) for i, (a, b, _) in enumerate(steps)]
    stores = [pltpu.make_async_copy(b, o, store.at[i]) for i, (_, b, o) in enumerate(steps)]
    for copy in loads:
        copy.start()
    for copy_in, copy_out in zip(loads, stores):
        copy_in.wait()
        copy_out.start()
    for copy in stores:
        copy.wait()


def fused(points, in_weight, slice_token_weight, cotangent):
    count = points.shape[0]
    vmem = pl.BlockSpec(memory_space=pltpu.VMEM)
    dma = pltpu.SemaphoreType.DMA
    hbm = pl.BlockSpec(memory_space=pl.ANY)
    out_shape = (
        jax.ShapeDtypeStruct((count, D), BF16),
        jax.ShapeDtypeStruct((ROWS, WIDTH), F32),
        jax.ShapeDtypeStruct((3, DH, DH), F32),
    )
    outs = pl.pallas_call(
        kernel,
        out_shape=out_shape,
        in_specs=[hbm, hbm, vmem, hbm],
        out_specs=(hbm, vmem, vmem),
        scratch_shapes=[
            pltpu.VMEM((count, D), BF16),
            pltpu.VMEM((count, D), BF16),
            pltpu.VMEM((count, D), BF16),
            pltpu.VMEM((N, ROWS, WIDTH), BF16),
            pltpu.VMEM((D, count), BF16),
            pltpu.VMEM((count, D), BF16),
            pltpu.VMEM((H * M, count), F32),
            pltpu.VMEM((H * M, count), BF16),
            pltpu.VMEM((N, 40, 128), F32),
            pltpu.VMEM((N, 40, 128), F32),
            pltpu.VMEM((N, 40, 128), F32),
            pltpu.VMEM((H * M, 256), BF16),
            pltpu.VMEM((H * M, 256), BF16),
            pltpu.VMEM((H * M, 128), F32),
            pltpu.VMEM((count, WIDTH), BF16),
            pltpu.VMEM((Z, 4 * ROWS, WIDTH), F32),
            pltpu.VMEM((Z, ROWS, WIDTH), F32),
            pltpu.VMEM((Z, 2, ROWS, WIDTH), BF16),
            pltpu.VMEM((Z, 2, ROWS, WIDTH), BF16),
            pltpu.VMEM((Z, ROWS, WIDTH), BF16),
            pltpu.VMEM((Z, ROWS, WIDTH), BF16),
            pltpu.VMEM((Z - 1, ROWS, WIDTH), BF16),
            pltpu.VMEM((Z - 1, ROWS, WIDTH), BF16),
            dma((3,)), dma((4,)), dma((4, N)), dma((N,)), dma((2, N)), dma((2, N)),
            dma((Z,)), dma((Z,)), dma((Z,)), dma((Z,)), dma((Z - 1,)), dma((Z - 1,)),
        ],
        compiler_params=pltpu.CompilerParams(
            collective_id=0, has_side_effects=True, vmem_limit_bytes=60 * 1024 * 1024
        ),
    )(points, in_weight, slice_token_weight, cotangent)
    return pl.pallas_call(
        hand_on,
        out_shape=out_shape,
        in_specs=[hbm] * 3,
        out_specs=(hbm,) * 3,
        scratch_shapes=[pltpu.VMEM(o.shape, o.dtype) for o in out_shape] + [dma((6,)), dma((6,))],
    )(*outs)


def solution(mesh):
    body = fused if mesh.shape["seq"] == N else local

    return jax.shard_map(
        body,
        mesh=mesh,
        in_specs=(P(("groups", "seq"), None), P("seq", None), P(), P(("groups", "seq"), None)),
        out_specs=(P(("groups", "seq"), None), P(("groups", "seq"), None), P("groups", None, None)),
        check_vma=False,
    )
```

```python
import jax
import jax.numpy as jnp
from jax import lax
from jax.experimental import pallas as pl
from jax.experimental.pallas import tpu as pltpu
from jax.sharding import PartitionSpec as P

D = 1024
H = 16
M = 32
DH = 64


def token_mixing(slice_tokens, slice_token_weight):
    highest_precision = lax.Precision.HIGHEST
    query_rows = jnp.einsum(
        "pat,tg->pag", slice_tokens, slice_token_weight[0], precision=highest_precision
    )
    key_matrix = jnp.einsum(
        "pat,tg->pag", slice_tokens, slice_token_weight[1], precision=highest_precision
    )
    value_matrix = jnp.einsum(
        "pat,tg->pag", slice_tokens, slice_token_weight[2], precision=highest_precision
    )
    scores = jnp.einsum(
        "hme,hke->hmk", query_rows, key_matrix, precision=highest_precision
    ) / jnp.sqrt(jnp.float32(DH))
    attend = jax.nn.softmax(scores, axis=-1)
    return jnp.einsum("hmk,hke->hme", attend, value_matrix, precision=highest_precision)


def local(points, in_weight, slice_token_weight, cotangent):
    count = points.shape[0]
    whole_weight = lax.all_gather(in_weight, "seq", axis=0, tiled=True)
    projected = jnp.dot(points, whole_weight, preferred_element_type=jnp.float32)
    point_features = projected[:, :D].astype(jnp.bfloat16).reshape(count, H, DH)
    soft = jax.nn.softmax(projected[:, D:].reshape(count, H, M), axis=-1)
    backward_softmax = soft.astype(jnp.bfloat16)
    backward_gradient = cotangent.reshape(count, H, DH)
    mass = jnp.sum(backward_softmax.astype(jnp.float32), axis=0)
    slice_totals = jnp.einsum(
        "uog,uoa->oga", backward_softmax, point_features, preferred_element_type=jnp.float32
    )
    mass, slice_totals = lax.psum((mass, slice_totals), "seq")
    denom = mass + 1e-05
    slice_tokens = slice_totals / denom[:, :, None]
    mixed, mix_vjp = jax.vjp(token_mixing, slice_tokens, slice_token_weight)
    backward_mixed_tokens = mixed.astype(jnp.bfloat16)
    local_mixed_tokens = jnp.einsum(
        "uog,uoa->oga", backward_softmax, backward_gradient, preferred_element_type=jnp.float32
    )
    mixed_tokens_gradient = lax.psum(local_mixed_tokens, "seq")
    d_tokens, grad_token_weights = mix_vjp(mixed_tokens_gradient)
    slice_totals_gradient = (d_tokens / denom[:, :, None]).astype(jnp.bfloat16)
    slice_mass_gradient = -jnp.sum(d_tokens * slice_tokens, axis=-1) / denom
    softmax_gradient = jnp.einsum(
        "ugv,gfv->ugf", backward_gradient, backward_mixed_tokens, preferred_element_type=jnp.float32
    )
    softmax_gradient = (
        softmax_gradient
        + jnp.einsum(
            "ugv,gfv->ugf",
            point_features,
            slice_totals_gradient,
            preferred_element_type=jnp.float32,
        )
        + slice_mass_gradient[None]
    )
    d_logits = soft * (softmax_gradient - jnp.sum(soft * softmax_gradient, axis=-1, keepdims=True))
    feature_gradient = jnp.einsum(
        "lvt,vtz->lvz", backward_softmax, slice_totals_gradient, preferred_element_type=jnp.float32
    )
    grads = jnp.concatenate(
        [feature_gradient.reshape(count, D), d_logits.reshape(count, H * M)], axis=1
    ).astype(jnp.bfloat16)
    back = lax.dot_general(
        grads, whole_weight, (((1,), (1,)), ((), ())), preferred_element_type=jnp.float32
    )
    grad_points = back.astype(jnp.bfloat16)
    grad_in_weight = lax.psum_scatter(
        lax.dot_general(
            points, grads, (((0,), (0,)), ((), ())), preferred_element_type=jnp.float32
        ),
        "seq",
        scatter_dimension=0,
        tiled=True,
    )
    return (grad_points, grad_in_weight, grad_token_weights)


MESH = pl.DeviceIdType.MESH
F32 = jnp.float32
BF16 = jnp.bfloat16
HIGHEST = lax.Precision.HIGHEST
N = 16
Z = 4
ROWS = D // N
WIDTH = D + H * M


def dot(a, b, dims=(1, 0), precision=None):
    return lax.dot_general(
        a, b, (((dims[0],), (dims[1],)), ((), ())), precision=precision, preferred_element_type=F32
    )


def kernel(
    points_hbm, win, tw, cot_hbm, gp_hbm, gw, gtw,
    points, cot, gp, w, pts_t, feat, soft, softb, stat, rbuf, full, dsum_m, mix_m, dmass, grads,
    sbuf, part, keep, cbuf, crbuf, ybuf, yrbuf, zbuf, zrbuf,
    load, store, gsend, grecv, ssend, srecv, csend, crecv, ysend, yrecv, zsend, zrecv,
):
    count = points.shape[0]
    tile = 256
    me = lax.axis_index("seq")
    z, y, c = me // 4, (me // 2) % 2, me % 2

    def device(zz, yy, cc):
        return (zz * 2 + yy) * 2 + cc

    sibling, across = device(z, y, 1 - c), device(z, 1 - y, c)

    def remote(src, dst, send, recv, to):
        return pltpu.make_async_remote_copy(
            src_ref=src, dst_ref=dst, send_sem=send, recv_sem=recv,
            device_id={"seq": to}, device_id_type=MESH,
        )

    barrier = pltpu.get_barrier_semaphore()

    @pl.loop(1, N)
    def _(k):
        pl.semaphore_signal(
            barrier, inc=1, device_id={"seq": lax.rem(me + k, N)}, device_id_type=MESH
        )

    loads = [
        pltpu.make_async_copy(win, w.at[me], load.at[0]),
        pltpu.make_async_copy(points_hbm, points, load.at[1]),
        pltpu.make_async_copy(cot_hbm, cot, load.at[2]),
    ]
    for copy in loads:
        copy.start()
    loads[0].wait()
    pl.semaphore_wait(barrier, N - 1)

    def block(blk, slot, to):
        return remote(w.at[blk], w.at[blk], gsend.at[slot, blk], grecv.at[blk], to)

    up = jnp.minimum(z + 1, Z - 1)
    down = jnp.maximum(z - 1, 0)
    to_up, to_down = device(up, y, c), device(down, y, c)

    def spread(blk):
        block(blk, 2, across).start()
        block(blk, 3, sibling).start()

    @pl.when(z < Z - 1)
    def _():
        block(me, 0, to_up).start()

    @pl.when(z > 0)
    def _():
        block(me, 1, to_down).start()

    spread(me)

    loads[1].wait()
    for k in range(D // tile):
        cols = slice(k * tile, (k + 1) * tile)
        pts_t[cols, :] = points[:, cols].T

    def partner(mask):
        return 2 * lax.rem(z // 2 + mask // 2, 2) + lax.rem(z + mask, 2)

    def forward(d):
        @pl.when(z - d >= 0)
        def _():
            blk = device(z - d, y, c)
            block(blk, 0, to_up).wait_recv()

            @pl.when(z < Z - 1)
            def _():
                block(blk, 0, to_up).start()

            spread(blk)

        @pl.when(z + d < Z)
        def _():
            blk = device(z + d, y, c)
            block(blk, 1, to_down).wait_recv()

            @pl.when(z > 0)
            def _():
                block(blk, 1, to_down).start()

            spread(blk)

    def plane_arrives(zz):
        blk = device(zz, 1 - y, c)
        block(blk, 2, across).wait_recv()
        block(blk, 3, sibling).start()
        for yy in range(2):
            block(device(zz, yy, 1 - c), 3, sibling).wait_recv()

    def plane_term(zz, rows):
        cols = pl.ds(pl.multiple_of(zz * 4 * ROWS, 4 * ROWS), 4 * ROWS)
        return dot(points[rows, cols], w[pl.ds(4 * zz, 4)].reshape(4 * ROWS, WIDTH))

    @pl.loop(0, Z - 1)
    def _(step):
        forward(step + 1)
        zz = partner(step)
        plane_arrives(zz)

        @pl.loop(0, count // tile)
        def _(t):
            term = plane_term(zz, pl.ds(pl.multiple_of(t * tile, tile), tile))

            @pl.when(step == 0)
            def _():
                part[t] = term

            @pl.when(step > 0)
            def _():
                part[t] += term

    plane_arrives(partner(Z - 1))
    loads[2].wait()

    @pl.loop(0, count // tile)
    def _(t):
        rows = pl.ds(pl.multiple_of(t * tile, tile), tile)
        projected = part[t] + plane_term(partner(Z - 1), rows)
        feat[rows, :] = projected[:, :D].astype(BF16)
        logits = projected[:, D:].T.reshape(H, M, tile)
        e = jnp.exp(logits - jnp.max(logits, axis=1, keepdims=True))
        s = (e / jnp.sum(e, axis=1, keepdims=True)).reshape(H * M, tile)
        soft[:, rows] = s
        softb[:, rows] = s.astype(BF16)

    ones = jnp.ones((8, count), BF16)
    for j in range(4):
        sl, fl = slice(128 * j, 128 * j + 128), slice(256 * j, 256 * j + 256)
        s = softb[sl, :]
        rf, rg = dot(s, feat[:, fl]), dot(s, cot[:, fl])
        mass = dot(ones, s, (1, 1))
        for hh in range(4):
            a, b = slice(32 * hh, 32 * hh + 32), slice(64 * hh, 64 * hh + 64)
            stat[hh % 2, 2 * j + hh // 2, 0:32, :] = jnp.concatenate([rf[a, b], rg[a, b]], axis=1)
            stat[hh % 2, 2 * j + hh // 2, 32:40, :] = mass

    half = N // 2
    q = me // 2
    halves = remote(stat.at[1 - c], sbuf, ssend.at[0, q], srecv.at[0, q], sibling)
    halves.start()
    halves.wait_recv()

    @pl.loop(0, half)
    def _(k):
        stat[c, k] += sbuf[k]

    def peer(k):
        return lax.rem(q + k, half)

    def piece(k):
        return remote(
            stat.at[c, k], rbuf.at[q], ssend.at[0, k], srecv.at[0, q], 2 * k + c
        )

    def landed(k):
        return remote(stat.at[c, k], rbuf.at[k], ssend.at[0, k], srecv.at[0, k], 2 * k + c)

    @pl.loop(1, half)
    def _(k):
        piece(peer(k)).start()

    rbuf[q] = stat[c, q]

    @pl.loop(1, half)
    def _(k):
        landed(peer(k)).wait_recv()

    full[c, q] = jnp.sum(rbuf[...], axis=0)

    def total(k):
        return remote(
            full.at[c, q], full.at[c, q], ssend.at[1, k], srecv.at[1, q], 2 * k + c
        )

    def total_landed(k):
        return remote(full.at[c, k], full.at[c, k], ssend.at[1, k], srecv.at[1, k], 2 * k + c)

    @pl.loop(1, half)
    def _(k):
        total(peer(k)).start()

    @pl.loop(1, half)
    def _(k):
        total_landed(peer(k)).wait_recv()

    whole = remote(full.at[c], full.at[c], ssend.at[1, q], srecv.at[1, q], sibling)
    whole.start()
    whole.wait_recv()

    wq, wk, wv = tw[0], tw[1], tw[2]
    row_head = lax.broadcasted_iota(jnp.int32, (128, 128), 0) // M
    col_head = lax.broadcasted_iota(jnp.int32, (128, 128), 1) // M
    same = row_head == col_head
    wide = (
        lax.broadcasted_iota(jnp.int32, (128, 256), 0) // M
        == lax.broadcasted_iota(jnp.int32, (128, 256), 1) // DH
    )
    groups = range(4)

    def heads_of(j, rows, lanes):
        return [full[hh % 2, 2 * j + hh // 2, rows, lanes] for hh in range(4)]

    def cut(x):
        return [x[128 * j : 128 * j + 128] for j in groups]

    def join(parts):
        return jnp.concatenate(parts, axis=0)

    def each(a, b, dims):
        return [dot(a[j], b[j], dims, HIGHEST) for j in groups]

    lanes_a, lanes_b = slice(0, DH), slice(DH, 2 * DH)
    sums = join([join(heads_of(j, slice(0, 32), lanes_a)) for j in groups])
    d_mixed = [join(heads_of(j, slice(0, 32), lanes_b)) for j in groups]
    denom = (
        join(
            [jnp.broadcast_to(full[0, 2 * j, 32:33, :], (128, 128)).T[:, :DH] for j in groups]
        )
        + 1e-05
    )
    tokens = sums / denom
    q_rows = cut(dot(tokens, wq, precision=HIGHEST))
    k_rows = cut(dot(tokens, wk, precision=HIGHEST))
    v_rows = cut(dot(tokens, wv, precision=HIGHEST))
    scores = each(q_rows, k_rows, (1, 1))
    d_attend = each(d_mixed, v_rows, (1, 1))
    attend = []
    for j in groups:
        shown = jnp.where(same, scores[j] * 0.125, -jnp.inf)
        e = jnp.exp(shown - jnp.max(shown, axis=1, keepdims=True))
        attend.append(e / jnp.sum(e, axis=1, keepdims=True))
    ds = []
    for j in groups:
        da = jnp.where(same, d_attend[j], 0.0)
        ds.append(attend[j] * (da - jnp.sum(attend[j] * da, axis=1, keepdims=True)) * 0.125)
    dq = join(each(ds, k_rows, (1, 0)))
    dk = join(each([x.T for x in ds], q_rows, (1, 0)))
    dv = join(each([x.T for x in attend], d_mixed, (1, 0)))
    mixed = each(attend, v_rows, (1, 0))
    d_tokens = (
        dot(dq, wq, (1, 1), HIGHEST)
        + dot(dk, wk, (1, 1), HIGHEST)
        + dot(dv, wv, (1, 1), HIGHEST)
    )
    d_sums = cut(d_tokens / denom)
    d_mass = cut(-jnp.sum(d_tokens * tokens, axis=1, keepdims=True) / denom[:, 0:1])
    for j in groups:
        sl = slice(128 * j, 128 * j + 128)
        mix_m[sl, :] = jnp.where(wide, jnp.concatenate([mixed[j]] * 4, axis=1), 0.0).astype(BF16)
        dsum_m[sl, :] = jnp.where(wide, jnp.concatenate([d_sums[j]] * 4, axis=1), 0.0).astype(BF16)
        dmass[sl, :] = jnp.broadcast_to(d_mass[j], (128, 128))
    gq = dot(tokens, dq, (0, 0), HIGHEST)
    gk = dot(tokens, dk, (0, 0), HIGHEST)
    gv = dot(tokens, dv, (0, 0), HIGHEST)
    gtw[0] = gq
    gtw[1] = gk
    gtw[2] = gv

    for j in range(4):
        sl, fl = slice(128 * j, 128 * j + 128), slice(256 * j, 256 * j + 256)
        d_soft = (
            dot(mix_m[sl, :], cot[:, fl], (1, 1))
            + dot(dsum_m[sl, :], feat[:, fl], (1, 1))
            + dmass[sl, 0:1]
        )
        s = soft[sl, :]
        inner = jnp.sum((s * d_soft).reshape(4, M, count), axis=1, keepdims=True)
        d_logits = s.reshape(4, M, count) * (d_soft.reshape(4, M, count) - inner)
        grads[:, D + 128 * j : D + 128 * j + 128] = d_logits.reshape(128, count).T.astype(BF16)
        grads[:, fl] = dot(softb[sl, :], dsum_m[sl, :], (0, 0)).astype(BF16)

    def to_core(u):
        return remote(cbuf.at[u], crbuf.at[u], csend.at[u], crecv.at[u], sibling)

    def to_across(u):
        return remote(ybuf.at[u], yrbuf.at[u], ysend.at[u], yrecv.at[u], across)

    def unit_owner(u):
        return partner(Z - 1 - u)

    def to_owner(u):
        to = partner(2) if u == 1 else partner(1)
        return remote(
            zbuf.at[u], zrbuf.at[u], zsend.at[u], zrecv.at[u], device(to, y, c)
        )

    unit = 4 * ROWS

    def core_step(u):
        to_core(u).wait_recv()
        theirs = pl.ds(pl.multiple_of((1 - y) * 2 * ROWS + c * ROWS, ROWS), ROWS)
        mine = pl.ds(pl.multiple_of(y * 2 * ROWS + c * ROWS, ROWS), ROWS)
        ybuf[u] = (part[u, theirs, :] + crbuf[u, 1 - y].astype(F32)).astype(BF16)
        to_across(u).start()
        keep[u] = part[u, mine, :] + crbuf[u, y].astype(F32)

    @pl.loop(0, Z)
    def _(u):
        rows = pl.ds(pl.multiple_of(unit_owner(u) * unit, unit), unit)
        part[u] = dot(pts_t[rows, :], grads[...])
        for yy in range(2):
            other = pl.ds(pl.multiple_of(yy * 2 * ROWS + (1 - c) * ROWS, ROWS), ROWS)
            cbuf[u, yy] = part[u, other, :].astype(BF16)
        to_core(u).start()

        @pl.when(u > 0)
        def _():
            core_step(u - 1)

    core_step(Z - 1)

    def gp_copy(t):
        rows = pl.ds(pl.multiple_of(t * tile, tile), tile)
        return pltpu.make_async_copy(gp.at[rows, :], gp_hbm.at[rows, :], store.at[t])

    def gp_tiles(start, stop):
        @pl.loop(start, stop)
        def _(t):
            rows = pl.ds(pl.multiple_of(t * tile, tile), tile)
            gp[rows, :] = dot(grads[rows, :], w[...].reshape(D, WIDTH), (1, 1)).astype(BF16)
            gp_copy(t).start()

    def summed(u):
        to_across(u).wait_recv()
        return keep[u] + yrbuf[u].astype(F32)

    tiles = count // tile
    gp_tiles(0, tiles // 2)
    zbuf[0] = summed(0).astype(BF16)
    to_owner(0).start()
    gp_tiles(tiles // 2, tiles)
    second = summed(1)
    to_owner(0).wait_recv()
    zbuf[1] = (second + zrbuf[0].astype(F32)).astype(BF16)
    to_owner(1).start()
    zbuf[2] = summed(2).astype(BF16)
    to_owner(2).start()
    own = summed(3)
    to_owner(1).wait_recv()
    own = own + zrbuf[1].astype(F32)
    to_owner(2).wait_recv()
    gw[...] = own + zrbuf[2].astype(F32)

    @pl.loop(0, tiles)
    def _(t):
        gp_copy(t).wait()

    for zz in range(Z):
        block(device(zz, y, c), 2, across).wait_send()
        for yy in range(2):
            block(device(zz, yy, c), 3, sibling).wait_send()

        @pl.when((z < Z - 1) & (zz <= z))
        def _():
            block(device(zz, y, c), 0, to_up).wait_send()

        @pl.when((z > 0) & (zz >= z))
        def _():
            block(device(zz, y, c), 1, to_down).wait_send()

    @pl.loop(1, N // 2)
    def _(k):
        piece(peer(k)).wait_send()
        total(peer(k)).wait_send()

    halves.wait_send()
    whole.wait_send()

    @pl.loop(0, Z)
    def _(u):
        to_core(u).wait_send()
        to_across(u).wait_send()

    for u in range(Z - 1):
        to_owner(u).wait_send()


def hand_on(gp, gw, gtw, gp_out, gw_out, gtw_out, gp_v, gw_v, gtw_v, load, store):
    size = gp.shape[0] // 4
    steps = [
        (gp.at[pl.ds(k * size, size)], gp_v.at[pl.ds(k * size, size)], gp_out.at[pl.ds(k * size, size)])
        for k in range(4)
    ]
    steps += [(gw, gw_v, gw_out), (gtw, gtw_v, gtw_out)]
    loads = [pltpu.make_async_copy(a, b, load.at[i]) for i, (a, b, _) in enumerate(steps)]
    stores = [pltpu.make_async_copy(b, o, store.at[i]) for i, (_, b, o) in enumerate(steps)]
    for copy in loads:
        copy.start()
    for copy_in, copy_out in zip(loads, stores):
        copy_in.wait()
        copy_out.start()
    for copy in stores:
        copy.wait()


def fused(points, in_weight, slice_token_weight, cotangent):
    count = points.shape[0]
    vmem = pl.BlockSpec(memory_space=pltpu.VMEM)
    dma = pltpu.SemaphoreType.DMA
    hbm = pl.BlockSpec(memory_space=pl.ANY)
    out_shape = (
        jax.ShapeDtypeStruct((count, D), BF16),
        jax.ShapeDtypeStruct((ROWS, WIDTH), F32),
        jax.ShapeDtypeStruct((3, DH, DH), F32),
    )
    outs = pl.pallas_call(
        kernel,
        out_shape=out_shape,
        in_specs=[hbm, hbm, vmem, hbm],
        out_specs=(hbm, vmem, vmem),
        scratch_shapes=[
            pltpu.VMEM((count, D), BF16),
            pltpu.VMEM((count, D), BF16),
            pltpu.VMEM((count, D), BF16),
            pltpu.VMEM((N, ROWS, WIDTH), BF16),
            pltpu.VMEM((D, count), BF16),
            pltpu.VMEM((count, D), BF16),
            pltpu.VMEM((H * M, count), F32),
            pltpu.VMEM((H * M, count), BF16),
            pltpu.VMEM((2, N // 2, 40, 128), F32),
            pltpu.VMEM((N // 2, 40, 128), F32),
            pltpu.VMEM((2, N // 2, 40, 128), F32),
            pltpu.VMEM((H * M, 256), BF16),
            pltpu.VMEM((H * M, 256), BF16),
            pltpu.VMEM((H * M, 128), F32),
            pltpu.VMEM((count, WIDTH), BF16),
            pltpu.VMEM((N // 2, 40, 128), F32),
            pltpu.VMEM((Z, 4 * ROWS, WIDTH), F32),
            pltpu.VMEM((Z, ROWS, WIDTH), F32),
            pltpu.VMEM((Z, 2, ROWS, WIDTH), BF16),
            pltpu.VMEM((Z, 2, ROWS, WIDTH), BF16),
            pltpu.VMEM((Z, ROWS, WIDTH), BF16),
            pltpu.VMEM((Z, ROWS, WIDTH), BF16),
            pltpu.VMEM((Z - 1, ROWS, WIDTH), BF16),
            pltpu.VMEM((Z - 1, ROWS, WIDTH), BF16),
            dma((3,)), dma((4,)), dma((4, N)), dma((N,)), dma((2, N)), dma((2, N)),
            dma((Z,)), dma((Z,)), dma((Z,)), dma((Z,)), dma((Z - 1,)), dma((Z - 1,)),
        ],
        compiler_params=pltpu.CompilerParams(
            collective_id=0, has_side_effects=True, vmem_limit_bytes=60 * 1024 * 1024
        ),
    )(points, in_weight, slice_token_weight, cotangent)
    return pl.pallas_call(
        hand_on,
        out_shape=out_shape,
        in_specs=[hbm] * 3,
        out_specs=(hbm,) * 3,
        scratch_shapes=[pltpu.VMEM(o.shape, o.dtype) for o in out_shape] + [dma((6,)), dma((6,))],
    )(*outs)


def solution(mesh):
    body = fused if mesh.shape["seq"] == N else local

    return jax.shard_map(
        body,
        mesh=mesh,
        in_specs=(P(("groups", "seq"), None), P("seq", None), P(), P(("groups", "seq"), None)),
        out_specs=(P(("groups", "seq"), None), P(("groups", "seq"), None), P("groups", None, None)),
        check_vma=False,
    )
```

```python
import jax
import jax.numpy as jnp
from jax import lax
from jax.experimental import pallas as pl
from jax.experimental.pallas import tpu as pltpu
from jax.sharding import PartitionSpec as P

D = 1024
H = 16
M = 32
DH = 64


def token_mixing(slice_tokens, slice_token_weight):
    highest_precision = lax.Precision.HIGHEST
    query_rows = jnp.einsum(
        "pat,tg->pag", slice_tokens, slice_token_weight[0], precision=highest_precision
    )
    key_matrix = jnp.einsum(
        "pat,tg->pag", slice_tokens, slice_token_weight[1], precision=highest_precision
    )
    value_matrix = jnp.einsum(
        "pat,tg->pag", slice_tokens, slice_token_weight[2], precision=highest_precision
    )
    scores = jnp.einsum(
        "hme,hke->hmk", query_rows, key_matrix, precision=highest_precision
    ) / jnp.sqrt(jnp.float32(DH))
    attend = jax.nn.softmax(scores, axis=-1)
    return jnp.einsum("hmk,hke->hme", attend, value_matrix, precision=highest_precision)


def local(points, in_weight, slice_token_weight, cotangent):
    count = points.shape[0]
    whole_weight = lax.all_gather(in_weight, "seq", axis=0, tiled=True)
    projected = jnp.dot(points, whole_weight, preferred_element_type=jnp.float32)
    point_features = projected[:, :D].astype(jnp.bfloat16).reshape(count, H, DH)
    soft = jax.nn.softmax(projected[:, D:].reshape(count, H, M), axis=-1)
    backward_softmax = soft.astype(jnp.bfloat16)
    backward_gradient = cotangent.reshape(count, H, DH)
    mass = jnp.sum(backward_softmax.astype(jnp.float32), axis=0)
    slice_totals = jnp.einsum(
        "uog,uoa->oga", backward_softmax, point_features, preferred_element_type=jnp.float32
    )
    mass, slice_totals = lax.psum((mass, slice_totals), "seq")
    denom = mass + 1e-05
    slice_tokens = slice_totals / denom[:, :, None]
    mixed, mix_vjp = jax.vjp(token_mixing, slice_tokens, slice_token_weight)
    backward_mixed_tokens = mixed.astype(jnp.bfloat16)
    local_mixed_tokens = jnp.einsum(
        "uog,uoa->oga", backward_softmax, backward_gradient, preferred_element_type=jnp.float32
    )
    mixed_tokens_gradient = lax.psum(local_mixed_tokens, "seq")
    d_tokens, grad_token_weights = mix_vjp(mixed_tokens_gradient)
    slice_totals_gradient = (d_tokens / denom[:, :, None]).astype(jnp.bfloat16)
    slice_mass_gradient = -jnp.sum(d_tokens * slice_tokens, axis=-1) / denom
    softmax_gradient = jnp.einsum(
        "ugv,gfv->ugf", backward_gradient, backward_mixed_tokens, preferred_element_type=jnp.float32
    )
    softmax_gradient = (
        softmax_gradient
        + jnp.einsum(
            "ugv,gfv->ugf",
            point_features,
            slice_totals_gradient,
            preferred_element_type=jnp.float32,
        )
        + slice_mass_gradient[None]
    )
    d_logits = soft * (softmax_gradient - jnp.sum(soft * softmax_gradient, axis=-1, keepdims=True))
    feature_gradient = jnp.einsum(
        "lvt,vtz->lvz", backward_softmax, slice_totals_gradient, preferred_element_type=jnp.float32
    )
    grads = jnp.concatenate(
        [feature_gradient.reshape(count, D), d_logits.reshape(count, H * M)], axis=1
    ).astype(jnp.bfloat16)
    back = lax.dot_general(
        grads, whole_weight, (((1,), (1,)), ((), ())), preferred_element_type=jnp.float32
    )
    grad_points = back.astype(jnp.bfloat16)
    grad_in_weight = lax.psum_scatter(
        lax.dot_general(
            points, grads, (((0,), (0,)), ((), ())), preferred_element_type=jnp.float32
        ),
        "seq",
        scatter_dimension=0,
        tiled=True,
    )
    return (grad_points, grad_in_weight, grad_token_weights)


MESH = pl.DeviceIdType.MESH
F32 = jnp.float32
BF16 = jnp.bfloat16
HIGHEST = lax.Precision.HIGHEST
N = 16
Z = 4
ROWS = D // N
WIDTH = D + H * M


def dot(a, b, dims=(1, 0), precision=None):
    return lax.dot_general(
        a, b, (((dims[0],), (dims[1],)), ((), ())), precision=precision, preferred_element_type=F32
    )


def kernel(
    points_hbm, win, tw, cot_hbm, gp_hbm, gw, gtw,
    points, cot, gp, w, pts_t, feat, soft, softb, stat, rbuf, full, dsum_m, mix_m, dmass, grads,
    sbuf, part, keep, cbuf, crbuf, ybuf, yrbuf, zbuf, zrbuf,
    load, store, gsend, grecv, ssend, srecv, csend, crecv, ysend, yrecv, zsend, zrecv,
):
    count = points.shape[0]
    tile = 256
    me = lax.axis_index("seq")
    z, y, c = me // 4, (me // 2) % 2, me % 2

    def device(zz, yy, cc):
        return (zz * 2 + yy) * 2 + cc

    sibling, across = device(z, y, 1 - c), device(z, 1 - y, c)

    def remote(src, dst, send, recv, to):
        return pltpu.make_async_remote_copy(
            src_ref=src, dst_ref=dst, send_sem=send, recv_sem=recv,
            device_id={"seq": to}, device_id_type=MESH,
        )

    barrier = pltpu.get_barrier_semaphore()

    @pl.loop(1, N)
    def _(k):
        pl.semaphore_signal(
            barrier, inc=1, device_id={"seq": lax.rem(me + k, N)}, device_id_type=MESH
        )

    g = lax.axis_index("groups")
    twin = {"groups": 1 - g, "seq": me}
    pl.semaphore_signal(barrier, inc=1, device_id=twin, device_id_type=MESH)

    loads = [
        pltpu.make_async_copy(win, w.at[me], load.at[0]),
        pltpu.make_async_copy(points_hbm, points, load.at[1]),
        pltpu.make_async_copy(cot_hbm, cot, load.at[2]),
    ]
    for copy in loads:
        copy.start()
    loads[0].wait()
    pl.semaphore_wait(barrier, N)

    def block(blk, slot, to):
        return remote(w.at[blk], w.at[blk], gsend.at[slot, blk], grecv.at[blk], to)

    up = jnp.minimum(z + 1, Z - 1)
    down = jnp.maximum(z - 1, 0)
    to_up, to_down = device(up, y, c), device(down, y, c)

    def over_y(zz):
        return lax.rem(zz, 2) == g

    def to_twin(blk):
        return pltpu.make_async_remote_copy(
            src_ref=w.at[blk], dst_ref=w.at[blk], send_sem=gsend.at[4, blk],
            recv_sem=grecv.at[blk], device_id=twin, device_id_type=MESH,
        )

    def spread(blk):
        @pl.when(over_y(blk // 4))
        def _():
            block(blk, 2, across).start()

        block(blk, 3, sibling).start()

    @pl.when(z < Z - 1)
    def _():
        block(me, 0, to_up).start()

    @pl.when(z > 0)
    def _():
        block(me, 1, to_down).start()

    spread(me)

    loads[1].wait()
    for k in range(D // tile):
        cols = slice(k * tile, (k + 1) * tile)
        pts_t[cols, :] = points[:, cols].T

    def partner(mask):
        return 2 * lax.rem(z // 2 + mask // 2, 2) + lax.rem(z + mask, 2)

    def forward(d):
        @pl.when(z - d >= 0)
        def _():
            blk = device(z - d, y, c)
            block(blk, 0, to_up).wait_recv()

            @pl.when(z < Z - 1)
            def _():
                block(blk, 0, to_up).start()

            spread(blk)

        @pl.when(z + d < Z)
        def _():
            blk = device(z + d, y, c)
            block(blk, 1, to_down).wait_recv()

            @pl.when(z > 0)
            def _():
                block(blk, 1, to_down).start()

            spread(blk)

    def plane_arrives(zz):
        blk = device(zz, 1 - y, c)
        block(blk, 2, across).wait_recv()

        @pl.when(over_y(zz))
        def _():
            to_twin(blk).start()

        block(blk, 3, sibling).start()
        for yy in range(2):
            block(device(zz, yy, 1 - c), 3, sibling).wait_recv()

    def plane_term(zz, rows):
        cols = pl.ds(pl.multiple_of(zz * 4 * ROWS, 4 * ROWS), 4 * ROWS)
        return dot(points[rows, cols], w[pl.ds(4 * zz, 4)].reshape(4 * ROWS, WIDTH))

    @pl.loop(0, Z - 1)
    def _(step):
        forward(step + 1)
        zz = partner(step)
        plane_arrives(zz)

        @pl.loop(0, count // tile)
        def _(t):
            term = plane_term(zz, pl.ds(pl.multiple_of(t * tile, tile), tile))

            @pl.when(step == 0)
            def _():
                part[t] = term

            @pl.when(step > 0)
            def _():
                part[t] += term

    plane_arrives(partner(Z - 1))
    loads[2].wait()

    @pl.loop(0, count // tile)
    def _(t):
        rows = pl.ds(pl.multiple_of(t * tile, tile), tile)
        projected = part[t] + plane_term(partner(Z - 1), rows)
        feat[rows, :] = projected[:, :D].astype(BF16)
        logits = projected[:, D:].T.reshape(H, M, tile)
        e = jnp.exp(logits - jnp.max(logits, axis=1, keepdims=True))
        s = (e / jnp.sum(e, axis=1, keepdims=True)).reshape(H * M, tile)
        soft[:, rows] = s
        softb[:, rows] = s.astype(BF16)

    ones = jnp.ones((8, count), BF16)
    for j in range(4):
        sl, fl = slice(128 * j, 128 * j + 128), slice(256 * j, 256 * j + 256)
        s = softb[sl, :]
        rf, rg = dot(s, feat[:, fl]), dot(s, cot[:, fl])
        mass = dot(ones, s, (1, 1))
        for hh in range(4):
            a, b = slice(32 * hh, 32 * hh + 32), slice(64 * hh, 64 * hh + 64)
            stat[hh % 2, 2 * j + hh // 2, 0:32, :] = jnp.concatenate([rf[a, b], rg[a, b]], axis=1)
            stat[hh % 2, 2 * j + hh // 2, 32:40, :] = mass

    half = N // 2
    q = me // 2
    halves = remote(stat.at[1 - c], sbuf, ssend.at[0, q], srecv.at[0, q], sibling)
    halves.start()
    halves.wait_recv()

    @pl.loop(0, half)
    def _(k):
        stat[c, k] += sbuf[k]

    def peer(k):
        return lax.rem(q + k, half)

    def piece(k):
        return remote(
            stat.at[c, k], rbuf.at[q], ssend.at[0, k], srecv.at[0, q], 2 * k + c
        )

    def landed(k):
        return remote(stat.at[c, k], rbuf.at[k], ssend.at[0, k], srecv.at[0, k], 2 * k + c)

    @pl.loop(1, half)
    def _(k):
        piece(peer(k)).start()

    rbuf[q] = stat[c, q]

    @pl.loop(1, half)
    def _(k):
        landed(peer(k)).wait_recv()

    full[c, q] = jnp.sum(rbuf[...], axis=0)

    def total(k):
        return remote(
            full.at[c, q], full.at[c, q], ssend.at[1, k], srecv.at[1, q], 2 * k + c
        )

    def total_landed(k):
        return remote(full.at[c, k], full.at[c, k], ssend.at[1, k], srecv.at[1, k], 2 * k + c)

    @pl.loop(1, half)
    def _(k):
        total(peer(k)).start()

    @pl.loop(1, half)
    def _(k):
        total_landed(peer(k)).wait_recv()

    whole = remote(full.at[c], full.at[c], ssend.at[1, q], srecv.at[1, q], sibling)
    whole.start()
    whole.wait_recv()

    wq, wk, wv = tw[0], tw[1], tw[2]
    row_head = lax.broadcasted_iota(jnp.int32, (128, 128), 0) // M
    col_head = lax.broadcasted_iota(jnp.int32, (128, 128), 1) // M
    same = row_head == col_head
    wide = (
        lax.broadcasted_iota(jnp.int32, (128, 256), 0) // M
        == lax.broadcasted_iota(jnp.int32, (128, 256), 1) // DH
    )
    groups = range(4)

    def heads_of(j, rows, lanes):
        return [full[hh % 2, 2 * j + hh // 2, rows, lanes] for hh in range(4)]

    def cut(x):
        return [x[128 * j : 128 * j + 128] for j in groups]

    def join(parts):
        return jnp.concatenate(parts, axis=0)

    def each(a, b, dims):
        return [dot(a[j], b[j], dims, HIGHEST) for j in groups]

    lanes_a, lanes_b = slice(0, DH), slice(DH, 2 * DH)
    sums = join([join(heads_of(j, slice(0, 32), lanes_a)) for j in groups])
    d_mixed = [join(heads_of(j, slice(0, 32), lanes_b)) for j in groups]
    denom = (
        join(
            [jnp.broadcast_to(full[0, 2 * j, 32:33, :], (128, 128)).T[:, :DH] for j in groups]
        )
        + 1e-05
    )
    tokens = sums / denom
    q_rows = cut(dot(tokens, wq, precision=HIGHEST))
    k_rows = cut(dot(tokens, wk, precision=HIGHEST))
    v_rows = cut(dot(tokens, wv, precision=HIGHEST))
    scores = each(q_rows, k_rows, (1, 1))
    d_attend = each(d_mixed, v_rows, (1, 1))
    attend = []
    for j in groups:
        shown = jnp.where(same, scores[j] * 0.125, -jnp.inf)
        e = jnp.exp(shown - jnp.max(shown, axis=1, keepdims=True))
        attend.append(e / jnp.sum(e, axis=1, keepdims=True))
    ds = []
    for j in groups:
        da = jnp.where(same, d_attend[j], 0.0)
        ds.append(attend[j] * (da - jnp.sum(attend[j] * da, axis=1, keepdims=True)) * 0.125)
    dq = join(each(ds, k_rows, (1, 0)))
    dk = join(each([x.T for x in ds], q_rows, (1, 0)))
    dv = join(each([x.T for x in attend], d_mixed, (1, 0)))
    mixed = each(attend, v_rows, (1, 0))
    d_tokens = (
        dot(dq, wq, (1, 1), HIGHEST)
        + dot(dk, wk, (1, 1), HIGHEST)
        + dot(dv, wv, (1, 1), HIGHEST)
    )
    d_sums = cut(d_tokens / denom)
    d_mass = cut(-jnp.sum(d_tokens * tokens, axis=1, keepdims=True) / denom[:, 0:1])
    for j in groups:
        sl = slice(128 * j, 128 * j + 128)
        mix_m[sl, :] = jnp.where(wide, jnp.concatenate([mixed[j]] * 4, axis=1), 0.0).astype(BF16)
        dsum_m[sl, :] = jnp.where(wide, jnp.concatenate([d_sums[j]] * 4, axis=1), 0.0).astype(BF16)
        dmass[sl, :] = jnp.broadcast_to(d_mass[j], (128, 128))
    gq = dot(tokens, dq, (0, 0), HIGHEST)
    gk = dot(tokens, dk, (0, 0), HIGHEST)
    gv = dot(tokens, dv, (0, 0), HIGHEST)
    gtw[0] = gq
    gtw[1] = gk
    gtw[2] = gv

    for j in range(4):
        sl, fl = slice(128 * j, 128 * j + 128), slice(256 * j, 256 * j + 256)
        d_soft = (
            dot(mix_m[sl, :], cot[:, fl], (1, 1))
            + dot(dsum_m[sl, :], feat[:, fl], (1, 1))
            + dmass[sl, 0:1]
        )
        s = soft[sl, :]
        inner = jnp.sum((s * d_soft).reshape(4, M, count), axis=1, keepdims=True)
        d_logits = s.reshape(4, M, count) * (d_soft.reshape(4, M, count) - inner)
        grads[:, D + 128 * j : D + 128 * j + 128] = d_logits.reshape(128, count).T.astype(BF16)
        grads[:, fl] = dot(softb[sl, :], dsum_m[sl, :], (0, 0)).astype(BF16)

    def to_core(u):
        return remote(cbuf.at[u], crbuf.at[u], csend.at[u], crecv.at[u], sibling)

    def to_across(u):
        return remote(ybuf.at[u], yrbuf.at[u], ysend.at[u], yrecv.at[u], across)

    def unit_owner(u):
        return partner(Z - 1 - u)

    def to_owner(u):
        to = partner(2) if u == 1 else partner(1)
        return remote(
            zbuf.at[u], zrbuf.at[u], zsend.at[u], zrecv.at[u], device(to, y, c)
        )

    unit = 4 * ROWS

    def core_step(u):
        to_core(u).wait_recv()
        theirs = pl.ds(pl.multiple_of((1 - y) * 2 * ROWS + c * ROWS, ROWS), ROWS)
        mine = pl.ds(pl.multiple_of(y * 2 * ROWS + c * ROWS, ROWS), ROWS)
        ybuf[u] = (part[u, theirs, :] + crbuf[u, 1 - y].astype(F32)).astype(BF16)
        to_across(u).start()
        keep[u] = part[u, mine, :] + crbuf[u, y].astype(F32)

    @pl.loop(0, Z)
    def _(u):
        rows = pl.ds(pl.multiple_of(unit_owner(u) * unit, unit), unit)
        part[u] = dot(pts_t[rows, :], grads[...])
        for yy in range(2):
            other = pl.ds(pl.multiple_of(yy * 2 * ROWS + (1 - c) * ROWS, ROWS), ROWS)
            cbuf[u, yy] = part[u, other, :].astype(BF16)
        to_core(u).start()

        @pl.when(u > 0)
        def _():
            core_step(u - 1)

    core_step(Z - 1)

    def gp_copy(t):
        rows = pl.ds(pl.multiple_of(t * tile, tile), tile)
        return pltpu.make_async_copy(gp.at[rows, :], gp_hbm.at[rows, :], store.at[t])

    def gp_tiles(start, stop):
        @pl.loop(start, stop)
        def _(t):
            rows = pl.ds(pl.multiple_of(t * tile, tile), tile)
            gp[rows, :] = dot(grads[rows, :], w[...].reshape(D, WIDTH), (1, 1)).astype(BF16)
            gp_copy(t).start()

    def summed(u):
        to_across(u).wait_recv()
        return keep[u] + yrbuf[u].astype(F32)

    tiles = count // tile
    gp_tiles(0, tiles // 2)
    zbuf[0] = summed(0).astype(BF16)
    to_owner(0).start()
    gp_tiles(tiles // 2, tiles)
    second = summed(1)
    to_owner(0).wait_recv()
    zbuf[1] = (second + zrbuf[0].astype(F32)).astype(BF16)
    to_owner(1).start()
    zbuf[2] = summed(2).astype(BF16)
    to_owner(2).start()
    own = summed(3)
    to_owner(1).wait_recv()
    own = own + zrbuf[1].astype(F32)
    to_owner(2).wait_recv()
    gw[...] = own + zrbuf[2].astype(F32)

    @pl.loop(0, tiles)
    def _(t):
        gp_copy(t).wait()

    for zz in range(Z):
        @pl.when(over_y(zz))
        def _():
            block(device(zz, y, c), 2, across).wait_send()
            to_twin(device(zz, 1 - y, c)).wait_send()

        for yy in range(2):
            block(device(zz, yy, c), 3, sibling).wait_send()

        @pl.when((z < Z - 1) & (zz <= z))
        def _():
            block(device(zz, y, c), 0, to_up).wait_send()

        @pl.when((z > 0) & (zz >= z))
        def _():
            block(device(zz, y, c), 1, to_down).wait_send()

    @pl.loop(1, N // 2)
    def _(k):
        piece(peer(k)).wait_send()
        total(peer(k)).wait_send()

    halves.wait_send()
    whole.wait_send()

    @pl.loop(0, Z)
    def _(u):
        to_core(u).wait_send()
        to_across(u).wait_send()

    for u in range(Z - 1):
        to_owner(u).wait_send()


def hand_on(gp, gw, gtw, gp_out, gw_out, gtw_out, gp_v, gw_v, gtw_v, load, store):
    size = gp.shape[0] // 4
    steps = [
        (gp.at[pl.ds(k * size, size)], gp_v.at[pl.ds(k * size, size)], gp_out.at[pl.ds(k * size, size)])
        for k in range(4)
    ]
    steps += [(gw, gw_v, gw_out), (gtw, gtw_v, gtw_out)]
    loads = [pltpu.make_async_copy(a, b, load.at[i]) for i, (a, b, _) in enumerate(steps)]
    stores = [pltpu.make_async_copy(b, o, store.at[i]) for i, (_, b, o) in enumerate(steps)]
    for copy in loads:
        copy.start()
    for copy_in, copy_out in zip(loads, stores):
        copy_in.wait()
        copy_out.start()
    for copy in stores:
        copy.wait()


def fused(points, in_weight, slice_token_weight, cotangent):
    count = points.shape[0]
    vmem = pl.BlockSpec(memory_space=pltpu.VMEM)
    dma = pltpu.SemaphoreType.DMA
    hbm = pl.BlockSpec(memory_space=pl.ANY)
    out_shape = (
        jax.ShapeDtypeStruct((count, D), BF16),
        jax.ShapeDtypeStruct((ROWS, WIDTH), F32),
        jax.ShapeDtypeStruct((3, DH, DH), F32),
    )
    outs = pl.pallas_call(
        kernel,
        out_shape=out_shape,
        in_specs=[hbm, hbm, vmem, hbm],
        out_specs=(hbm, vmem, vmem),
        scratch_shapes=[
            pltpu.VMEM((count, D), BF16),
            pltpu.VMEM((count, D), BF16),
            pltpu.VMEM((count, D), BF16),
            pltpu.VMEM((N, ROWS, WIDTH), BF16),
            pltpu.VMEM((D, count), BF16),
            pltpu.VMEM((count, D), BF16),
            pltpu.VMEM((H * M, count), F32),
            pltpu.VMEM((H * M, count), BF16),
            pltpu.VMEM((2, N // 2, 40, 128), F32),
            pltpu.VMEM((N // 2, 40, 128), F32),
            pltpu.VMEM((2, N // 2, 40, 128), F32),
            pltpu.VMEM((H * M, 256), BF16),
            pltpu.VMEM((H * M, 256), BF16),
            pltpu.VMEM((H * M, 128), F32),
            pltpu.VMEM((count, WIDTH), BF16),
            pltpu.VMEM((N // 2, 40, 128), F32),
            pltpu.VMEM((Z, 4 * ROWS, WIDTH), F32),
            pltpu.VMEM((Z, ROWS, WIDTH), F32),
            pltpu.VMEM((Z, 2, ROWS, WIDTH), BF16),
            pltpu.VMEM((Z, 2, ROWS, WIDTH), BF16),
            pltpu.VMEM((Z, ROWS, WIDTH), BF16),
            pltpu.VMEM((Z, ROWS, WIDTH), BF16),
            pltpu.VMEM((Z - 1, ROWS, WIDTH), BF16),
            pltpu.VMEM((Z - 1, ROWS, WIDTH), BF16),
            dma((3,)), dma((4,)), dma((5, N)), dma((N,)), dma((2, N)), dma((2, N)),
            dma((Z,)), dma((Z,)), dma((Z,)), dma((Z,)), dma((Z - 1,)), dma((Z - 1,)),
        ],
        compiler_params=pltpu.CompilerParams(
            collective_id=0, has_side_effects=True, vmem_limit_bytes=60 * 1024 * 1024
        ),
    )(points, in_weight, slice_token_weight, cotangent)
    return pl.pallas_call(
        hand_on,
        out_shape=out_shape,
        in_specs=[hbm] * 3,
        out_specs=(hbm,) * 3,
        scratch_shapes=[pltpu.VMEM(o.shape, o.dtype) for o in out_shape] + [dma((6,)), dma((6,))],
    )(*outs)


def solution(mesh):
    body = fused if mesh.shape["seq"] == N and mesh.shape["groups"] == 2 else local

    return jax.shard_map(
        body,
        mesh=mesh,
        in_specs=(P(("groups", "seq"), None), P("seq", None), P(), P(("groups", "seq"), None)),
        out_specs=(P(("groups", "seq"), None), P(("groups", "seq"), None), P("groups", None, None)),
        check_vma=False,
    )
```
